256 devices in a mesh: dp: 4 (over x), expert: 64 (over y, z, core).
Axes of the slice: x: 4, y: 4, z: 8, core: 2. Of those that a mesh axis runs over, the one named last changes fastest.
Arguments:
- tokens: bfloat16 [8192, 4096], P('expert', 'dp'), may hold values from -6 to 6
- expert_ids: int32 [8192, 2], P('expert'), may hold values from 0 to 63, all different within a row; in each aligned block of 128 rows (0 to 127, 128 to 255, ...) at most 5 rows name the same one
- route_weights: float32 [8192, 2], P('expert'), may hold values from 0.1 to 1
- w_gate: bfloat16 [14336, 4096], P('expert', 'dp'), may hold values from -0.09375 to 0.09375
- w_up: bfloat16 [14336, 4096], P('expert', 'dp'), may hold values from -0.09375 to 0.09375
- w_down: bfloat16 [14336, 4096], P('expert', 'dp'), may hold values from -0.125 to 0.125
- out_grad: bfloat16 [8192, 4096], P('expert', 'dp'), may hold values from -0.59765625 to 0.59765625
Outputs:
- output: bfloat16 [8192, 4096], P('expert', 'dp')
- grad_gate: bfloat16 [14336, 4096], P('expert', 'dp')
- grad_up: bfloat16 [14336, 4096], P('expert', 'dp')
- grad_down: bfloat16 [14336, 4096], P('expert', 'dp')
The draws below stay inside these ranges and needn't reach their ends.
Inputs may be any that keep to these rules, and one draw needn't show every extreme that they name: `expert_ids`: each token names two different experts. Among the 128 tokens of one index of expert (aligned blocks of 128 rows), no expert is named more than 5 times, a bound that some block reaches.
All inputs are finite; a program needn't handle non-finite values.
Results may differ from the reference program's by a relative error of at most 0.029.
Values may be sent and summed in bfloat16 or wider, within the bound.
A program may use at most 128 MiB of HBM per device.

```python
import math
import jax
import jax.numpy as jnp
import numpy as np
from jax import lax

D = 4096
FF = 14336
SLICES = 8
TOK_DEV = 128
H = 1792
EXPERTS = 64
COPIES = 8
FEAT_BLOCKS = 4
CAP = 5
ROWS = 320
TOKENS = 8192


def block_levels(stream_key, shape, split, smallest, top_value):
    def one(dim, blocks):
        heights = jax.random.uniform(jax.random.fold_in(jax.random.fold_in(stream_key, 6), dim), (blocks,), jnp.float32, smallest / len(split), top_value / len(split))
        return jnp.repeat(jnp.exp(heights), shape[dim] // blocks).reshape((-1,) + (1,) * (len(shape) - dim - 1))

    gain = one(*split[0])
    for cut in split[1:]:
        gain = gain * one(*cut)
    return gain


def assign_block(rng, own, number, rows, number_of, top, reach, slope):
    sequence = jax.random.permutation(rng, number_of)
    heavy_load, ordinary = load_shares(number_of, rows * top, reach, slope, True), load_shares(number_of, rows * top, reach, slope, False)
    places = jnp.arange(number_of)

    def named(sizes, offset_by):
        used = int((sizes > 0).sum())
        fixed = max(1, used // 4)
        moved = fixed + (places - fixed + offset_by * (used - fixed)) % max(1, number_of - fixed)
        return jnp.zeros((number_of,), jnp.int32).at[sequence[jnp.where(places < fixed, places, moved)]].set(jnp.asarray(sizes, jnp.int32))

    sizes = jnp.where(number % 4 == 0, named(heavy_load, number // 4), named(ordinary, number - number // 4 - 1))
    mixed = jax.random.permutation(jax.random.fold_in(own, 3), number_of)
    source_of, sink = mixed[0:number_of // 2 * 2:2], mixed[1:number_of // 2 * 2:2]
    room = jnp.minimum(sizes[source_of] - 1, reach - sizes[sink]) // 2
    room = jnp.where((source_of == sequence[0]) | (sink == sequence[0]) | (sizes[sink] == 0), 0, jnp.maximum(room, 0))
    moved = jax.random.randint(jax.random.fold_in(own, 4), (number_of // 2,), 0, 1 << 20) % (room + 1)
    sizes = sizes.at[source_of].add(-moved).at[sink].add(moved)
    labels = jnp.searchsorted(jnp.cumsum(sizes), jnp.arange(rows * top), side="right").astype(jnp.int32)
    table = labels.reshape(top, rows).T
    table = table[jax.random.permutation(jax.random.fold_in(own, 1), rows)]
    offset_by = jax.random.randint(jax.random.fold_in(own, 2), (rows, 1), 0, top)
    return jnp.take_along_axis(table, (jnp.arange(top)[None, :] + offset_by) % top, axis=1)


def load_shares(count, total, limit, lean, full):
    loads = [(1 << 20) // math.isqrt(standing ** lean) + 1 for standing in range(1, count + 1)]
    largest = limit if full else min(limit, max(-(-total // count), total * loads[0] // sum(loads)))
    least = 1 if total - largest >= count - 1 else 0
    given, spare = [largest] + [least] * (count - 1), total - largest - least * (count - 1)
    while spare > 0:
        free = [i for i in range(1, count) if given[i] < largest] or [i for i in range(1, count) if given[i] < limit]
        whole, left = sum([loads[i] for i in free]), spare
        for i in free:
            addition = min(limit - given[i], max(1, left * loads[i] // whole), spare)
            given[i] = given[i] + addition
            spare = spare - addition
    return np.array(given)


def noise(own_key, shape, spread, limit, pieces=(), held_as=jnp.bfloat16):
    level = block_levels(own_key, shape, pieces, -0.22, 0.18) if pieces else 1.0
    drawn = jax.random.normal(own_key, shape, jnp.float32) * spread * level
    return jnp.minimum(jnp.maximum(drawn, -limit), limit).astype(held_as)


def setup_inputs(seed: int = 0) -> dict:
    key_list = jax.random.split(jax.random.key(seed), 8)
    tokens = noise(key_list[0], (TOKENS, D), 1.0, 6.0, ((0, 64), (1, 4)))
    expert_ids_keys = jax.random.split(jax.random.fold_in(key_list[1], 1), TOKENS // TOK_DEV)
    expert_ids_turns = jax.random.permutation(jax.random.fold_in(key_list[1], 3), TOKENS // TOK_DEV)
    expert_ids = jax.vmap(lambda own, number: assign_block(jax.random.fold_in(key_list[1], 2), own, number, TOK_DEV, EXPERTS, 2, CAP, 2))(expert_ids_keys, expert_ids_turns).reshape((TOKENS, 2))
    route_weights = jnp.clip(0.1 + 0.9 * jax.random.uniform(key_list[2], (TOKENS, 2), jnp.float32) ** block_levels(key_list[2], (TOKENS, 2), ((0, 64),), -0.2, 0.2), 0.1, 1.0)
    w_gate = noise(key_list[3], (FF, D), D ** -0.5, 0.09375, ((0, 64), (1, 4)))
    w_up = noise(key_list[4], (FF, D), D ** -0.5, 0.09375, ((0, 64), (1, 4)))
    w_down = noise(key_list[5], (FF, D), H ** -0.5, 0.125, ((0, 64), (1, 4)))
    out_grad = noise(key_list[6], (TOKENS, D), 0.1, 0.59765625, ((0, 64), (1, 4)))
    return dict(tokens=tokens, expert_ids=expert_ids, route_weights=route_weights, w_gate=w_gate, w_up=w_up, w_down=w_down, out_grad=out_grad)


def silu_parts(gate_sum):
    gate_sigmoid = jax.nn.sigmoid(gate_sum)
    return gate_sum * gate_sigmoid, gate_sigmoid * (1.0 + gate_sum * (1.0 - gate_sigmoid))


def blocked(left_rows, right_mat, blocks):
    row_count = left_rows.shape[0]
    feat_count = left_rows.shape[1]
    left_blocks = left_rows.astype(jnp.float32).reshape(row_count, blocks, feat_count // blocks)
    right_blocks = right_mat.astype(jnp.float32).reshape(blocks, feat_count // blocks, right_mat.shape[1])
    partials = jnp.einsum("rqd,qdh->qrh", left_blocks, right_blocks)
    rounded = lax.optimization_barrier(partials.astype(jnp.bfloat16))
    return jnp.sum(rounded.astype(jnp.float32), axis=0)


def tree_sum(stacked):
    while stacked.shape[0] > 1:
        stacked = (stacked[0::2].astype(jnp.float32) + stacked[1::2].astype(jnp.float32)).astype(jnp.bfloat16)
    return stacked[0]


def one_expert(expert, gate_w, up_w, down_w, tokens, flat_ids, flat_weights, out_grad):
    chosen = flat_ids == expert
    picked_rows = jnp.nonzero(chosen, size=ROWS, fill_value=0)[0].astype(jnp.int32)
    is_live = jnp.arange(ROWS, dtype=jnp.int32) < jnp.sum(chosen.astype(jnp.int32))
    tok_index = picked_rows // 2
    gathered = jnp.where(is_live[:, None], tokens[tok_index], jnp.zeros((), jnp.bfloat16))
    gate_sum = blocked(gathered, gate_w.T, FEAT_BLOCKS)
    up_sum = blocked(gathered, up_w.T, FEAT_BLOCKS)
    active, slope_term = silu_parts(gate_sum)
    hidden = (active * up_sum).astype(jnp.bfloat16)
    expert_rows = jnp.dot(hidden, down_w, preferred_element_type=jnp.float32).astype(jnp.bfloat16)
    scale_rows = jnp.where(is_live, flat_weights[picked_rows], jnp.zeros((), jnp.float32))
    cot_rows = (scale_rows[:, None] * out_grad[tok_index].astype(jnp.float32)).astype(jnp.bfloat16)
    grad_hidden = blocked(cot_rows, down_w.T, FEAT_BLOCKS)
    grad_gate_rows = (grad_hidden * up_sum * slope_term).astype(jnp.bfloat16)
    grad_up_rows = (grad_hidden * active).astype(jnp.bfloat16)
    gate_term = jnp.dot(grad_gate_rows.T, gathered, preferred_element_type=jnp.float32).astype(jnp.bfloat16)
    up_term = jnp.dot(grad_up_rows.T, gathered, preferred_element_type=jnp.float32).astype(jnp.bfloat16)
    down_term = jnp.dot(hidden.T, cot_rows, preferred_element_type=jnp.float32).astype(jnp.bfloat16)
    return expert_rows, picked_rows, is_live, gate_term, up_term, down_term


def reference(tokens, expert_ids, route_weights, w_gate, w_up, w_down, out_grad):
    flat_ids = expert_ids.reshape(-1)
    flat_weights = route_weights.reshape(-1)

    def per_slice(slice_index):
        offset = (slice_index * H).astype(jnp.int32)
        gate_w = lax.dynamic_slice_in_dim(w_gate, offset, H, 0)
        up_w = lax.dynamic_slice_in_dim(w_up, offset, H, 0)
        down_w = lax.dynamic_slice_in_dim(w_down, offset, H, 0)

        def per_copy(copy_index):
            return one_expert(slice_index * COPIES + copy_index, gate_w, up_w, down_w, tokens, flat_ids, flat_weights, out_grad)

        rows_out, picked_all, live_all, gate_terms, up_terms, down_terms = lax.map(per_copy, jnp.arange(COPIES, dtype=jnp.int32))
        return rows_out, picked_all, live_all, tree_sum(gate_terms), tree_sum(up_terms), tree_sum(down_terms)

    results = lax.map(per_slice, jnp.arange(SLICES, dtype=jnp.int32))
    expert_rows = results[0].reshape(EXPERTS * ROWS, D)
    targets = jnp.where(results[2].reshape(-1), results[1].reshape(-1), 2 * TOKENS).astype(jnp.int32)
    assigned = jnp.zeros((2 * TOKENS, D), jnp.bfloat16).at[targets].set(expert_rows, mode="drop")
    combined = jnp.sum(route_weights[:, :, None] * assigned.reshape(TOKENS, 2, D).astype(jnp.float32), axis=1)
    output = combined.astype(jnp.bfloat16)
    grad_gate = results[3].reshape(FF, D)
    grad_up = results[4].reshape(FF, D)
    grad_down = results[5].reshape(FF, D)
    return (output, grad_gate, grad_up, grad_down)
```

```python
import jax
import jax.numpy as jnp
from jax import lax
from jax.experimental import pallas as pl
from jax.experimental.pallas import tpu as pltpu
from jax.sharding import PartitionSpec as P

NX, NY, NZ = 4, 4, 8
SLICES = 8
SLOT = 40
CODE = 64
TOK = 128
PER_Y = NZ * SLOT
ROWS = NY * PER_Y
CHUNK = 256
NCH = ROWS // CHUNK
WINDOW = 48
PIECES = ((0, 32, 0, 1), (32, 80, 0, 3), (112, 80, 2, 3), (192, 80, 4, 3), (272, 48, 6, 2))
PLACE = (0, 1, 3, 5, 7, 6, 4, 2)
MESH = pl.DeviceIdType.MESH
BF = jnp.bfloat16
F32 = jnp.float32
CROSS_LAST = (((1,), (1,)), ((), ()))
CROSS_FIRST = (((0,), (0,)), ((), ()))
PLAIN = (((1,), (0,)), ((), ()))


def dot(a, b, dims):
    return lax.dot_general(a, b, dims, preferred_element_type=F32)


def layer_kernel(
    tok_in, og_in, meta_in, wg, wu, wd,
    out, g_gate, g_up, g_down,
    w, meta, tb, gb, tx, cx, ts, cs,
    part, part_in, hid, part_h, part_h_in, grads_x,
    up_s, act_s, slope_s, rows_out, rows_back,
    ring_out, ring_in, acc, pair_out, pair_in,
    w_loc, w_send, w_recv, m_send, m_recv, own_sem,
    tz_send, tz_recv, gz_send, gz_recv, ty_send, ty_recv, cy_send, cy_recv,
    p_send, p_recv, h_send, h_recv, ph_send, ph_recv, gx_send, gx_recv,
    o_send, o_recv, r_send, r_recv, pair_send, pair_recv,
):
    own_h, feats = wg.shape
    half_f = feats // 2
    chip_h = 2 * own_h
    quarter_h = chip_h // NX
    x = lax.axis_index("dp")
    e = lax.axis_index("expert")
    c = lax.rem(e, 2)
    chip = e // 2
    z = lax.rem(chip, NZ)
    y = chip // NZ
    half = z // 4
    sibling = e + 1 - 2 * c

    def chip_at(dy, dz):
        return (x, (lax.rem(y + dy, NY) * NZ + lax.rem(z + dz, NZ)) * 2 + c)

    def x_peer(k):
        return lax.rem(x + k, NX)

    def remote(src, dst, send_sem, recv_sem, dev):
        return pltpu.make_async_remote_copy(
            src_ref=src, dst_ref=dst, send_sem=send_sem, recv_sem=recv_sem,
            device_id=dev, device_id_type=MESH)

    def wait_bytes(ref, sem):
        pltpu.make_async_copy(ref, ref, sem).wait()

    barrier = pltpu.get_barrier_semaphore()
    friends = [chip_at(0, d) for d in range(1, NZ)] + [chip_at(d, 0) for d in range(1, NY)]
    friends += [(x_peer(k), e) for k in range(1, NX)] + [(x, sibling)]
    for dev in friends:
        pl.semaphore_signal(barrier, inc=1, device_id=dev, device_id_type=MESH)
    pl.semaphore_wait(barrier, len(friends))

    def ring_send(own, buf, send, recv, k):
        for d in range(2):
            if k == 1:
                src, dst = own, buf.at[1 + d]
            else:
                src, dst = buf.at[2 * k - 3 + d], buf.at[2 * k - 1 + d if k < 4 else 7]
            if k == 4:
                lanes = pl.ds(d * half_f, half_f)
                src, dst = src.at[:, lanes], dst.at[:, lanes]
            remote(src, dst, send.at[d, k - 1], recv.at[d, k - 1], chip_at(0, 1 if d == 0 else NZ - 1)).start()

    def ring_wait(buf, recv, k):
        for d in range(2):
            ref = buf.at[1 + d] if k < 4 else buf.at[7, :, pl.ds(d * half_f, half_f)]
            wait_bytes(ref, recv.at[d, k - 1])

    pltpu.make_async_copy(tok_in, tb.at[0], own_sem.at[0]).start()
    for d in range(1, NZ):
        remote(meta_in, meta.at[PLACE[d]], m_send, m_recv, chip_at(0, d)).start()
    pltpu.make_async_copy(meta_in, meta.at[0], own_sem.at[2]).start()
    ring_send(tok_in, tb, tz_send, tz_recv, 1)
    pltpu.make_async_copy(og_in, gb.at[0], own_sem.at[1]).start()

    def w_part(i, core):
        return w.at[i, pl.ds(pl.multiple_of(core * own_h, 16), own_h)]

    for i, src in enumerate((wg, wu, wd)):
        remote(src, w_part(i, c), w_send.at[i], w_recv.at[i], (x, sibling)).start()
        pltpu.make_async_copy(src, w_part(i, c), w_loc.at[i]).start()

    wait_bytes(meta.at[0], own_sem.at[2])
    wait_bytes(meta.at[pl.ds(1, NZ - 1)], m_recv)

    def hits(dy, place, first, count):
        codes = meta[place, 0:2, :] - ((lax.rem(y + dy, NY) * 2 + half) * CODE).astype(F32)
        at = jnp.where((codes >= 0.0) & (codes < float(SLOT)), codes + float(place * SLOT), -1.0)
        row = (lax.broadcasted_iota(jnp.int32, (count, TOK), 0) + first).astype(F32)
        return row == at[0:1], row == at[1:2]

    def weights(dy, place, first, count):
        hit0, hit1 = hits(dy, place, first, count)
        return (jnp.where(hit0, meta[place, 2:3, :], 0.0) + jnp.where(hit1, meta[place, 3:4, :], 0.0))

    def select(p, buf, near, staged, send, recv, scaled):
        first, count, place, places = PIECES[p]
        wts = [[weights(dy, place + n, first, count) for n in range(places)] for dy in range(NY)]
        wts = jnp.concatenate([jnp.concatenate(r, axis=1) for r in wts], axis=0)
        picked = dot((wts > 0.0).astype(BF), buf[place:place + places].reshape(places * TOK, feats), PLAIN)
        if scaled:
            picked = jnp.sum(wts, axis=1, keepdims=True) * picked
        picked = picked.astype(BF)
        near[first:first + count] = picked[0:count]
        for dy in (1, 3, 2):
            staged[dy - 1, first:first + count] = picked[dy * count:(dy + 1) * count]
            remote(staged.at[dy - 1, pl.ds(first, count)],
                   near.at[pl.ds(dy * PER_Y + first, count)],
                   send.at[dy - 1], recv.at[dy - 1], chip_at(dy, 0)).start()

    def relay_step(k, own, buf, zs, zr, near, staged, ys, yr, scaled):
        ring_wait(buf, zr, k)
        if k < 4:
            ring_send(own, buf, zs, zr, k + 1)
        select(k, buf, near, staged, ys, yr, scaled)

    tok_args = (tok_in, tb, tz_send, tz_recv, tx, ts, ty_send, ty_recv, False)
    cot_args = (og_in, gb, gz_send, gz_recv, cx, cs, cy_send, cy_recv, True)
    wait_bytes(tb.at[0], own_sem.at[0])
    select(0, tb, tx, ts, ty_send, ty_recv, False)
    for k in range(1, 4):
        relay_step(k, *tok_args)
    ring_send(og_in, gb, gz_send, gz_recv, 1)
    relay_step(4, *tok_args)
    wait_bytes(gb.at[0], own_sem.at[1])
    select(0, gb, cx, cs, cy_send, cy_recv, True)

    def to_peers(src_of, dst, send, recv):
        for k in range(1, NX):
            x2 = x_peer(k)
            remote(src_of(x2), dst, send, recv, (x2, e)).start()

    def chunk(ref, i):
        start = i * CHUNK
        if not isinstance(i, int):
            start = pl.multiple_of(start, CHUNK)
        return ref[pl.ds(start, CHUNK)]

    def up_gate(i):
        rows = chunk(tx, i)
        for kind in range(2):
            prod = dot(w[kind], rows, CROSS_LAST).astype(BF)
            for q in range(NX):
                part[q, i, kind] = prod[q * quarter_h:(q + 1) * quarter_h]
        to_peers(lambda x2: part.at[x2, i], part_in.at[x, i], p_send.at[i], p_recv.at[i])

    def act(i):
        wait_bytes(part_in.at[pl.ds(0, NX - 1), i], p_recv.at[i])
        gate = part[x, i, 0].astype(F32)
        up = part[x, i, 1].astype(F32)
        for k in range(1, NX):
            gate += part_in[x_peer(k), i, 0].astype(F32)
            up += part_in[x_peer(k), i, 1].astype(F32)
        sig = jax.nn.sigmoid(gate)
        active = gate * sig
        up_s[i] = up
        act_s[i] = active
        slope_s[i] = sig * (1.0 + gate * (1.0 - sig))
        hid[i, x] = (active * up).astype(BF)
        to_peers(lambda x2: hid.at[i, x], hid.at[i, x], h_send.at[i], h_recv.at[i])

    def expert_out(i):
        wait_bytes(hid.at[i, pl.ds(0, NX - 1)], h_recv.at[i])
        rows_out[pl.ds(pl.multiple_of(i * CHUNK, CHUNK), CHUNK)] = dot(
            hid[i].reshape(chip_h, CHUNK), w[2], CROSS_FIRST).astype(BF)

    def hidden_part(i):
        prod = dot(w[2], chunk(cx, i), CROSS_LAST).astype(BF)
        for q in range(NX):
            part_h[q, i] = prod[q * quarter_h:(q + 1) * quarter_h]
        to_peers(lambda x2: part_h.at[x2, i], part_h_in.at[x, i], ph_send.at[i], ph_recv.at[i])

    def grad_rows(i):
        wait_bytes(part_h_in.at[pl.ds(0, NX - 1), i], ph_recv.at[i])
        gh = part_h[x, i].astype(F32)
        for k in range(1, NX):
            gh += part_h_in[x_peer(k), i].astype(F32)
        grads_x[i, x, 0] = (gh * up_s[i] * slope_s[i]).astype(BF)
        grads_x[i, x, 1] = (gh * act_s[i]).astype(BF)
        to_peers(lambda x2: grads_x.at[i, x], grads_x.at[i, x], gx_send.at[i], gx_recv.at[i])

    def down_step(i):
        acc[2] += dot(hid[i].reshape(chip_h, CHUNK), chunk(cx, i), PLAIN)

    def gate_step(i):
        wait_bytes(grads_x.at[i, pl.ds(0, NX - 1)], gx_recv.at[i])
        for kind in range(2):
            acc[kind] += dot(grads_x[i, :, kind].reshape(chip_h, CHUNK), chunk(tx, i), PLAIN)

    def loop(lo, hi, f):
        lax.fori_loop(lo, hi, lambda i, carry: (f(i), carry)[1], 0)

    def wait_rows(ref, recv, dy):
        wait_bytes(ref.at[pl.ds(dy * PER_Y, PER_Y)], recv.at[dy - 1])

    relay_step(1, *cot_args)
    for i, src in enumerate((wg, wu, wd)):
        wait_bytes(w_part(i, c), w_loc.at[i])
        wait_bytes(w_part(i, 1 - c), w_recv.at[i])
    up_gate(0)
    relay_step(2, *cot_args)
    wait_rows(tx, ty_recv, 1)
    wait_rows(tx, ty_recv, 3)
    wait_rows(tx, ty_recv, 2)
    loop(1, NCH, up_gate)
    relay_step(3, *cot_args)
    relay_step(4, *cot_args)
    loop(0, NCH, act)
    loop(0, NCH, expert_out)

    def give_back(p):
        first, count = PIECES[p][:2]
        for dy in (1, 3, 2):
            remote(rows_out.at[pl.ds(dy * PER_Y + first, count)],
                   rows_back.at[dy - 1, pl.ds(first, count)],
                   o_send.at[p], o_recv.at[p], chip_at(NY - dy, 0)).start()

    for p in (4, 3, 2, 1, 0):
        give_back(p)

    def await_piece(p):
        first, count = PIECES[p][:2]
        wait_bytes(rows_back.at[:, pl.ds(first, count)], o_recv.at[p])

    def dense(place):
        first = place * SLOT // 16 * 16
        rows = [rows_out[first:first + WINDOW]]
        rows += [rows_back[dy - 1, first:first + WINDOW] for dy in range(1, NY)]
        rows = jnp.concatenate(rows, axis=0)
        wts = jnp.concatenate([weights(dy, place, first, WINDOW) for dy in range(NY)], axis=0)
        coarse = wts.astype(BF)
        fine = (wts - coarse.astype(F32)).astype(BF)
        return dot(coarse, rows, CROSS_FIRST) + dot(fine, rows, CROSS_FIRST)

    def fold_send(k, d):
        src, dst = ring_out.at[d, k - 1], ring_in.at[d, k - 1]
        if k == 1:
            lanes = pl.ds(d * half_f, half_f)
            src, dst = src.at[:, lanes], dst.at[:, lanes]
        remote(src, dst, r_send.at[d, k - 1], r_recv.at[d, k - 1], chip_at(0, 1 if d == 0 else NZ - 1)).start()

    def fold_first():
        block = dense(7).astype(BF)
        for d in range(2):
            ring_out[d, 0] = block
            fold_send(1, d)

    def fold_wait(k, d):
        ref = ring_in.at[d, k - 1]
        wait_bytes(ref.at[:, pl.ds(d * half_f, half_f)] if k == 1 else ref, r_recv.at[d, k - 1])

    def fold(k):
        for d in range(2):
            block = dense(10 - 2 * k - d)
            fold_wait(k - 1, d)
            if k == 2:
                lanes = slice(d * half_f, (d + 1) * half_f)
                others = slice((1 - d) * half_f, (2 - d) * half_f)
                ring_out[d, 1, :, lanes] = (block[:, lanes] + ring_in[d, 0, :, lanes].astype(F32)).astype(BF)
                ring_out[d, 1, :, others] = block[:, others].astype(BF)
            else:
                ring_out[d, k - 1] = (block + ring_in[d, k - 2].astype(F32)).astype(BF)
            fold_send(k, d)

    for dy in (1, 3, 2):
        wait_rows(cx, cy_recv, dy)
    loop(0, NCH, hidden_part)
    acc[...] = jnp.zeros_like(acc)
    loop(0, NCH, grad_rows)
    await_piece(4)
    fold_first()
    loop(0, NCH, down_step)

    def send_pair(kind):
        pair_out[kind] = acc[kind, pl.ds(pl.multiple_of((1 - c) * own_h, 16), own_h)].astype(BF)
        remote(pair_out.at[kind], pair_in.at[kind], pair_send.at[kind], pair_recv.at[kind],
               (x, sibling)).start()

    send_pair(2)
    await_piece(3)
    fold(2)
    loop(0, 2, gate_step)
    await_piece(2)
    fold(3)
    loop(2, 4, gate_step)
    await_piece(1)
    fold(4)
    loop(4, NCH, gate_step)
    send_pair(0)
    send_pair(1)
    await_piece(0)
    mine = dense(0)

    def join_pair(kind, dest):
        wait_bytes(pair_in.at[kind], pair_recv.at[kind])
        dest[...] = (acc[kind, pl.ds(pl.multiple_of(c * own_h, 16), own_h)]
                     + pair_in[kind].astype(F32)).astype(BF)

    join_pair(2, g_down)
    join_pair(0, g_gate)
    join_pair(1, g_up)
    for d in range(2):
        fold_wait(4, d)
        mine += ring_in[d, 3].astype(F32)
    out[...] = mine.astype(BF)

    for i in range(3):
        wait_bytes(wg, w_send.at[i])
        wait_bytes(pair_out.at[i], pair_send.at[i])
    wait_bytes(meta.at[pl.ds(1, NZ - 1)], m_send)
    for d in range(2):
        lanes = pl.ds(d * half_f, half_f)
        for k in range(1, 5):
            for buf, sem in ((tb, tz_send), (gb, gz_send)):
                wait_bytes(buf.at[0] if k < 4 else buf.at[0, :, lanes], sem.at[d, k - 1])
            wait_bytes(ring_out.at[d, k - 1] if k > 1 else ring_out.at[d, 0, :, lanes], r_send.at[d, k - 1])
    for dy in range(1, NY):
        wait_bytes(ts.at[dy - 1], ty_send.at[dy - 1])
        wait_bytes(cs.at[dy - 1], cy_send.at[dy - 1])
    for p in range(5):
        wait_bytes(rows_back.at[:, pl.ds(0, PIECES[p][1])], o_send.at[p])
    for i in range(NCH):
        wait_bytes(part.at[pl.ds(0, NX - 1), i], p_send.at[i])
        wait_bytes(hid.at[i, pl.ds(0, NX - 1)], h_send.at[i])
        wait_bytes(part_h.at[pl.ds(0, NX - 1), i], ph_send.at[i])
        wait_bytes(grads_x.at[i, pl.ds(0, NX - 1)], gx_send.at[i])


def run_layer(tokens, out_grad, meta, wg, wu, wd):
    own_h, feats = wg.shape
    qh = 2 * own_h // NX
    dma = pltpu.SemaphoreType.DMA
    vm = pltpu.VMEM
    scratch = [
        vm((3, 2 * own_h, feats), BF), vm((NZ, 8, TOK), F32),
        vm((NZ, TOK, feats), BF), vm((NZ, TOK, feats), BF),
        vm((ROWS, feats), BF), vm((ROWS, feats), BF),
        vm((NY - 1, PER_Y, feats), BF), vm((NY - 1, PER_Y, feats), BF),
        vm((NX, NCH, 2, qh, CHUNK), BF), vm((NX, NCH, 2, qh, CHUNK), BF),
        vm((NCH, NX, qh, CHUNK), BF),
        vm((NX, NCH, qh, CHUNK), BF), vm((NX, NCH, qh, CHUNK), BF),
        vm((NCH, NX, 2, qh, CHUNK), BF),
        vm((NCH, qh, CHUNK), F32), vm((NCH, qh, CHUNK), F32), vm((NCH, qh, CHUNK), F32),
        vm((ROWS, feats), BF), vm((NY - 1, PER_Y, feats), BF),
        vm((2, 4, TOK, feats), BF), vm((2, 4, TOK, feats), BF),
        vm((3, 2 * own_h, feats), F32),
        vm((3, own_h, feats), BF), vm((3, own_h, feats), BF),
        dma((3,)), dma((3,)), dma((3,)), dma, dma, dma((3,)),
        dma((2, 4)), dma((2, 4)), dma((2, 4)), dma((2, 4)),
        dma((NY - 1,)), dma((NY - 1,)), dma((NY - 1,)), dma((NY - 1,)),
        dma((NCH,)), dma((NCH,)), dma((NCH,)), dma((NCH,)),
        dma((NCH,)), dma((NCH,)), dma((NCH,)), dma((NCH,)),
        dma((5,)), dma((5,)), dma((2, 4)), dma((2, 4)),
        dma((3,)), dma((3,)),
    ]
    anywhere = pl.BlockSpec(memory_space=pl.ANY)
    inside = pl.BlockSpec(memory_space=pltpu.VMEM)
    return pl.pallas_call(
        layer_kernel,
        out_shape=(
            jax.ShapeDtypeStruct((TOK, feats), BF),
            jax.ShapeDtypeStruct((own_h, feats), BF),
            jax.ShapeDtypeStruct((own_h, feats), BF),
            jax.ShapeDtypeStruct((own_h, feats), BF),
        ),
        in_specs=[anywhere] * 6,
        out_specs=[inside] * 4,
        scratch_shapes=scratch,
        compiler_params=pltpu.CompilerParams(
            collective_id=0, has_side_effects=True, vmem_limit_bytes=60 * 1024 * 1024),
    )(tokens, out_grad, meta, wg, wu, wd)


def per_device(tokens, expert_ids, route_weights, w_gate, w_up, w_down, out_grad):
    tok_rows = tokens.shape[0]
    slices = expert_ids // 8
    flat = slices.reshape(2 * tok_rows)
    choose = (flat[:, None] == jnp.arange(SLICES, dtype=jnp.int32)[None, :]).astype(jnp.int32)
    before = jnp.cumsum(choose, axis=0) - choose
    slot = jnp.sum(before * choose, axis=1).reshape(tok_rows, 2)
    code = (slices * CODE + slot).astype(F32)
    meta = jnp.concatenate([code.T, route_weights.T, jnp.zeros((4, tok_rows), F32)], axis=0)
    return run_layer(tokens, out_grad, meta, w_gate, w_up, w_down)


def solution(mesh):
    placed = (
        P("expert", "dp"),
        P("expert", None),
        P("expert", None),
        P("expert", "dp"),
        P("expert", "dp"),
        P("expert", "dp"),
        P("expert", "dp"),
    )
    return jax.shard_map(
        per_device,
        mesh=mesh,
        in_specs=placed,
        out_specs=(P("expert", "dp"), P("expert", "dp"), P("expert", "dp"), P("expert", "dp")),
        check_vma=False,
    )
```

```python
import jax
import jax.numpy as jnp
from jax import lax
from jax.experimental import pallas as pl
from jax.experimental.pallas import tpu as pltpu
from jax.sharding import PartitionSpec as P

NX, NY, NZ = 4, 4, 8
SLICES = 8
SLOT = 40
CODE = 64
TOK = 128
PER_Y = NZ * SLOT
ROWS = NY * PER_Y
GROUP = 64
CHUNK = NY * GROUP
NCH = PER_Y // GROUP
WINDOW = 48
TILE = 256
STEP, EARLY = 80, 48
BACK = ((272, 48), (192, 80), (112, 80), (32, 80), (0, 32))
PLACE = (0, 1, 3, 5, 7, 6, 4, 2)
MESH = pl.DeviceIdType.MESH
BF = jnp.bfloat16
F32 = jnp.float32
CROSS_LAST = (((1,), (1,)), ((), ()))
CROSS_FIRST = (((0,), (0,)), ((), ()))
PLAIN = (((1,), (0,)), ((), ()))


def dot(a, b, dims):
    return lax.dot_general(a, b, dims, preferred_element_type=F32)


def layer_kernel(
    tok_in, og_in, ids, route, wg, wu, wd,
    out, g_gate, g_up, g_down,
    w, meta, src_rows, xc, staged, hit_s, scale_s,
    part, part_in, mid, hid, part_h, part_h_in, mid_h, grads_x,
    up_s, act_s, slope_s, rows_out, rows_back,
    back_w, sum_s, ring_out, ring_in, acc, pair_out, pair_in,
    w_loc, w_send, w_recv, m_send, m_recv, own_sem,
    z_send, z_recv, y_send, y_recv,
    pm_send, pm_recv, p_send, p_recv, h_send, h_recv, h2_send, h2_recv,
    hm_send, hm_recv, ph_send, ph_recv, gx_send, gx_recv, g2_send, g2_recv,
    o_send, o_recv, r_send, r_recv, pair_send, pair_recv,
):
    own_h, feats = wg.shape
    half_f = feats // 2
    chip_h = 2 * own_h
    quarter_h = chip_h // NX
    x = lax.axis_index("dp")
    e = lax.axis_index("expert")
    c = lax.rem(e, 2)
    chip = e // 2
    z = lax.rem(chip, NZ)
    y = chip // NZ
    half = z // 4
    sibling = e + 1 - 2 * c

    def chip_at(dy, dz):
        return (x, (lax.rem(y + dy, NY) * NZ + lax.rem(z + dz, NZ)) * 2 + c)

    def x_peer(k):
        return lax.rem(x + k, NX)

    def remote(src, dst, send_sem, recv_sem, dev):
        return pltpu.make_async_remote_copy(
            src_ref=src, dst_ref=dst, send_sem=send_sem, recv_sem=recv_sem,
            device_id=dev, device_id_type=MESH)

    def wait_bytes(ref, sem):
        pltpu.make_async_copy(ref, ref, sem).wait()

    def set_meta():
        slices = lax.div(ids[...], 8)
        number = lax.broadcasted_iota(jnp.int32, (SLICES, TOK), 0)
        hit0 = (slices[0:1] == number).astype(F32)
        hit1 = (slices[1:2] == number).astype(F32)
        earlier = (lax.broadcasted_iota(jnp.int32, (TOK, TOK), 0)
                   < lax.broadcasted_iota(jnp.int32, (TOK, TOK), 1)).astype(F32).astype(BF)
        before = dot((hit0 + hit1).astype(BF), earlier, PLAIN)
        code = slices.astype(F32) * float(CODE)
        meta[0, 0:1] = code[0:1] + jnp.sum(hit0 * before, axis=0, keepdims=True)
        meta[0, 1:2] = code[1:2] + jnp.sum(hit1 * (before + hit0), axis=0, keepdims=True)
        meta[0, 2:4] = route[...]
        meta[0, 4:8] = jnp.zeros((4, TOK), F32)
        meta[NZ] = jnp.full((8, TOK), -1.0, F32)

    def each(count, f):
        lax.fori_loop(0, count, lambda i, carry: (f(i), carry)[1], 0)

    def blank(row):
        for a in range(2):
            src_rows[a, NZ, pl.ds(pl.multiple_of(row * 16, 16), 16)] = jnp.zeros((16, feats), BF)
            ring_in[a, 0, pl.ds(pl.multiple_of(row * 16, 16), 16), (1 - a) * half_f:(2 - a) * half_f] = (
                jnp.zeros((16, half_f), BF))

    def clear(row):
        for kind in range(3):
            acc[kind, pl.ds(pl.multiple_of(row * 16, 16), 16)] = jnp.zeros((16, feats), F32)

    def weights(dy, place, first, count):
        codes = meta[place, 0:2, :] - ((lax.rem(y + dy, NY) * 2 + half) * CODE).astype(F32)
        start = jnp.asarray(place * SLOT, jnp.int32).astype(F32)
        at = jnp.where((codes >= 0.0) & (codes < float(SLOT)), codes + start, -1.0)
        row = (lax.broadcasted_iota(jnp.int32, (count, TOK), 0) + first).astype(F32)
        return (jnp.where(row == at[0:1], meta[place, 2:3, :], 0.0)
                + jnp.where(row == at[1:2], meta[place, 3:4, :], 0.0))

    def spans(first, count):
        found, row = [], first
        while row < first + count:
            i = row // GROUP
            n = min(first + count, (i + 1) * GROUP) - row
            found.append((i, row - i * GROUP, row, n))
            row += n
        return found

    def choose(a, first, count, place, places):
        def one_y(dy):
            wts = jnp.concatenate([weights(dy, place + n, first, count) for n in range(places)], axis=1)
            here = pl.ds(pl.multiple_of(dy * count, 16), count)
            hit_s[here, 0:places * TOK] = (wts > 0.0).astype(F32).astype(BF)
            total = jnp.sum(wts, axis=1, keepdims=True)
            scale_s[here] = jnp.broadcast_to(jnp.where(a == 1, total, jnp.ones_like(total)), (count, TOK))

        def tile(n):
            lanes = pl.ds(pl.multiple_of(n * TILE, TILE), TILE)
            rows = src_rows[a, pl.ds(place, places), :, lanes].reshape(places * TOK, TILE)
            picked = dot(hit_s[0:NY * count, 0:places * TOK], rows, PLAIN)
            picked = (scale_s[0:NY * count, 0:1] * picked).astype(BF)
            for dy in range(NY):
                staged[a, dy, pl.ds(pl.multiple_of(first, 16), count), lanes] = picked[dy * count:(dy + 1) * count]

        each(NY, one_y)
        each(feats // TILE, tile)

    barrier = pltpu.get_barrier_semaphore()
    friends = [chip_at(0, d) for d in range(1, NZ)] + [chip_at(d, 0) for d in range(1, NY)]
    friends += [(x_peer(k), e) for k in range(1, NX)] + [(x, sibling)]
    for dev in friends:
        pl.semaphore_signal(barrier, inc=1, device_id=dev, device_id_type=MESH)
    pltpu.make_async_copy(tok_in, src_rows.at[0, 0], own_sem.at[0]).start()
    pltpu.make_async_copy(og_in, src_rows.at[1, 0], own_sem.at[1]).start()
    set_meta()
    for a in range(2):
        wait_bytes(src_rows.at[a, 0], own_sem.at[a])
    each(2, lambda a: choose(a, 0, 32, 0, 1))
    pl.semaphore_wait(barrier, len(friends))

    def ring_send(a, k, own=None):
        for d in range(2):
            if k == 1:
                src, dst = own, src_rows.at[a, 1 + d]
            else:
                src, dst = src_rows.at[a, 2 * k - 3 + d], src_rows.at[a, 2 * k - 1 + d if k < 4 else 7]
            if k == 4:
                lanes = pl.ds(d * half_f, half_f)
                src, dst = src.at[:, lanes], dst.at[:, lanes]
            remote(src, dst, z_send.at[a, d, k - 1], z_recv.at[a, d, k - 1],
                   chip_at(0, 1 if d == 0 else NZ - 1)).start()

    def ring_wait(a, k):
        for d in range(2):
            ref = src_rows.at[a, 2 * k - 1 + d] if k < 4 else src_rows.at[a, 7, :, pl.ds(d * half_f, half_f)]
            wait_bytes(ref, z_recv.at[a, d, k - 1])

    ring_send(0, 1, tok_in)
    for d in range(1, NZ):
        remote(meta.at[0], meta.at[PLACE[d]], m_send, m_recv, chip_at(0, d)).start()

    def w_part(i, core):
        return w.at[i, pl.ds(pl.multiple_of(core * own_h, 16), own_h)]

    def pass_on(a, first, count):
        for dy in (1, 3, 2):
            for i, off, row, n in spans(first, count):
                remote(staged.at[a, dy, pl.ds(row, n)], xc.at[a, i, dy, pl.ds(off, n)],
                       y_send.at[a, dy - 1], y_recv.at[a, i], chip_at(dy, 0)).start()
        for i, off, row, n in spans(first, count):
            pltpu.make_async_copy(staged.at[a, 0, pl.ds(row, n)], xc.at[a, i, 0, pl.ds(off, n)],
                                  y_recv.at[a, i]).start()

    def relay_step(a, k):
        for j in range(1, 5):
            @pl.when(k == j)
            def _(j=j):
                ring_wait(a, j)
                if j < 4:
                    ring_send(a, j + 1)
        choose(a, STEP * k - EARLY, STEP, 2 * k - 2, 3)
        for j in range(1, 5):
            @pl.when(k == j)
            def _(j=j):
                pass_on(a, STEP * j - EARLY, min(STEP, PER_Y - STEP * j + EARLY))

    left, far, right = x_peer(NX - 1), x_peer(2), x_peer(1)
    near_half, far_half = pl.ds(0, CHUNK // 2), pl.ds(CHUNK // 2, CHUNK // 2)

    def both_sides(rightward, leftward, send, recv, i):
        for d, (src, dst) in enumerate((rightward, leftward)):
            remote(src, dst, send.at[d, i], recv.at[d, i], ((right, left)[d], e)).start()

    def add_to(ref, extra):
        ref[...] = (ref[...].astype(F32) + extra.astype(F32)).astype(BF)

    def chunk(ref, i):
        return xc[ref, i].reshape(CHUNK, feats)

    def up_gate(i):
        rows = chunk(0, i)

        def one(kind):
            prod = dot(w[kind], rows, CROSS_LAST).astype(BF)
            for q in range(NX):
                part[q, i, kind] = prod[q * quarter_h:(q + 1) * quarter_h]

        each(2, one)
        both_sides((part.at[far, i, 0], mid.at[0, i]), (part.at[far, i, 1], mid.at[1, i]), pm_send, pm_recv, i)

    def up_gate_mid(i):
        wait_bytes(mid.at[0, i], pm_recv.at[0, i])
        wait_bytes(mid.at[1, i], pm_recv.at[1, i])
        add_to(part.at[right, i, 0], mid[0, i])
        add_to(part.at[left, i, 1], mid[1, i])
        both_sides((part.at[right, i], part_in.at[0, i]), (part.at[left, i], part_in.at[1, i]), p_send, p_recv, i)

    def act(i):
        for d in range(2):
            wait_bytes(part_in.at[d, i], p_recv.at[d, i])
        gate = part[x, i, 0].astype(F32)
        up = part[x, i, 1].astype(F32)
        for d in range(2):
            gate += part_in[d, i, 0].astype(F32)
            up += part_in[d, i, 1].astype(F32)
        sig = jax.nn.sigmoid(gate)
        active = gate * sig
        up_s[i] = up
        act_s[i] = active
        slope_s[i] = sig * (1.0 + gate * (1.0 - sig))
        hid[i, x] = (active * up).astype(BF)
        both_sides((hid.at[i, x], hid.at[i, x]), (hid.at[i, x], hid.at[i, x]), h_send, h_recv, i)

    def hid_pass(i):
        wait_bytes(hid.at[i, left], h_recv.at[0, i])
        wait_bytes(hid.at[i, right], h_recv.at[1, i])
        both_sides((hid.at[i, left, :, near_half],) * 2, (hid.at[i, right, :, far_half],) * 2, h2_send, h2_recv, i)

    def expert_out(i):
        wait_bytes(hid.at[i, far, :, near_half], h2_recv.at[0, i])
        wait_bytes(hid.at[i, far, :, far_half], h2_recv.at[1, i])
        prod = dot(hid[i].reshape(chip_h, CHUNK), w[2], CROSS_FIRST).astype(BF)
        rows_back[0, pl.ds(pl.multiple_of(i * GROUP, GROUP), GROUP)] = prod[0:GROUP]
        for dy in range(1, NY):
            rows_out[i, dy - 1] = prod[dy * GROUP:(dy + 1) * GROUP]

    def hidden_part(i):
        prod = dot(w[2], chunk(1, i), CROSS_LAST).astype(BF)
        for q in range(NX):
            part_h[q, i] = prod[q * quarter_h:(q + 1) * quarter_h]
        both_sides((part_h.at[far, i, :, near_half], mid_h.at[0, i]),
                   (part_h.at[far, i, :, far_half], mid_h.at[1, i]), hm_send, hm_recv, i)

    def hidden_mid(i):
        wait_bytes(mid_h.at[0, i], hm_recv.at[0, i])
        wait_bytes(mid_h.at[1, i], hm_recv.at[1, i])
        add_to(part_h.at[right, i, :, near_half], mid_h[0, i])
        add_to(part_h.at[left, i, :, far_half], mid_h[1, i])
        both_sides((part_h.at[right, i], part_h_in.at[0, i]), (part_h.at[left, i], part_h_in.at[1, i]),
                   ph_send, ph_recv, i)

    def grad_rows(i):
        for d in range(2):
            wait_bytes(part_h_in.at[d, i], ph_recv.at[d, i])
        gh = part_h[x, i].astype(F32)
        for d in range(2):
            gh += part_h_in[d, i].astype(F32)
        grads_x[i, x, 0] = (gh * up_s[i] * slope_s[i]).astype(BF)
        grads_x[i, x, 1] = (gh * act_s[i]).astype(BF)
        both_sides((grads_x.at[i, x],) * 2, (grads_x.at[i, x],) * 2, gx_send, gx_recv, i)

    def grads_pass(i):
        wait_bytes(grads_x.at[i, left], gx_recv.at[0, i])
        wait_bytes(grads_x.at[i, right], gx_recv.at[1, i])
        both_sides((grads_x.at[i, left, 0],) * 2, (grads_x.at[i, right, 1],) * 2, g2_send, g2_recv, i)

    def down_step(i):
        acc[2] += dot(hid[i].reshape(chip_h, CHUNK), chunk(1, i), PLAIN)

    def gate_step(i):
        wait_bytes(grads_x.at[i, far, 0], g2_recv.at[0, i])
        wait_bytes(grads_x.at[i, far, 1], g2_recv.at[1, i])

        def one(kind):
            acc[kind] += dot(grads_x[i, :, kind].reshape(chip_h, CHUNK), chunk(0, i), PLAIN)

        each(2, one)

    def give_back(first, count, g):
        for dy in (1, 3, 2):
            for i, off, row, n in spans(first, count):
                remote(rows_out.at[i, dy - 1, pl.ds(off, n)], rows_back.at[dy, pl.ds(row, n)],
                       o_send.at[g], o_recv.at[g], chip_at(NY - dy, 0)).start()

    def await_back(g):
        first, count = BACK[g]
        wait_bytes(rows_back.at[pl.ds(1, NY - 1), pl.ds(first, count)], o_recv.at[g])

    def dense(place):
        first = pl.multiple_of(place * SLOT // 16 * 16, 16)

        def one_y(dy):
            wts = weights(dy, place, first, WINDOW)
            coarse = wts.astype(BF)
            here = pl.ds(pl.multiple_of(dy * WINDOW, 16), WINDOW)
            back_w[0, here] = coarse
            back_w[1, here] = (wts - coarse.astype(F32)).astype(BF)

        def tile(n):
            lanes = pl.ds(pl.multiple_of(n * TILE, TILE), TILE)
            rows = rows_back[:, pl.ds(first, WINDOW), lanes].reshape(NY * WINDOW, TILE)
            sum_s[:, lanes] = dot(back_w[0], rows, CROSS_FIRST) + dot(back_w[1], rows, CROSS_FIRST)

        each(NY, one_y)
        each(feats // TILE, tile)

    def fold_send(k, d):
        src, dst = ring_out.at[d, k - 1], ring_in.at[d, k - 1]
        if k == 1:
            lanes = pl.ds(d * half_f, half_f)
            src, dst = src.at[:, lanes], dst.at[:, lanes]
        remote(src, dst, r_send.at[d, k - 1], r_recv.at[d, k - 1], chip_at(0, 1 if d == 0 else NZ - 1)).start()

    def fold_wait(k, d):
        ref = ring_in.at[d, k - 1]
        wait_bytes(ref.at[:, pl.ds(d * half_f, half_f)] if k == 1 else ref, r_recv.at[d, k - 1])

    def fold(n):
        for j, groups in ((0, (0,)), (1, (1,)), (3, (2,)), (5, (3,)), (7, (4,))):
            @pl.when(n == j)
            def _(groups=groups):
                for g in groups:
                    await_back(g)
        dense(7 - n)

        @pl.when(n == 0)
        def _():
            for d in range(2):
                ring_out[d, 0] = sum_s[...].astype(BF)
                fold_send(1, d)

        for j in range(1, 7):
            @pl.when(n == j)
            def _(k=(j + 3) // 2, d=(j - 1) % 2):
                fold_wait(k - 1, d)

        @pl.when((n >= 1) & (n <= 6))
        def _():
            k = (n + 3) // 2
            d = lax.rem(n - 1, 2)
            ring_out[d, k - 1] = (sum_s[...] + ring_in[d, k - 2].astype(F32)).astype(BF)

        for j in range(1, 7):
            @pl.when(n == j)
            def _(k=(j + 3) // 2, d=(j - 1) % 2):
                fold_send(k, d)

    def send_pair(kind):
        pair_out[kind] = acc[kind, pl.ds(pl.multiple_of((1 - c) * own_h, 16), own_h)].astype(BF)
        remote(pair_out.at[kind], pair_in.at[kind], pair_send.at[kind], pair_recv.at[kind],
               (x, sibling)).start()

    def join_pair(kind, dest):
        wait_bytes(pair_in.at[kind], pair_recv.at[kind])
        dest[...] = (acc[kind, pl.ds(pl.multiple_of(c * own_h, 16), own_h)]
                     + pair_in[kind].astype(F32)).astype(BF)

    def tok_chunk(i):
        wait_bytes(xc.at[0, i], y_recv.at[0, i])
        up_gate(i)

    def cot_chunk(i):
        wait_bytes(xc.at[1, i], y_recv.at[1, i])
        hidden_part(i)

    def weights_here():
        for i, src in enumerate((wg, wu, wd)):
            wait_bytes(w_part(i, c), w_loc.at[i])
            wait_bytes(w_part(i, 1 - c), w_recv.at[i])

    for a in range(2):
        pass_on(a, 0, 32)
    for i, src in enumerate((wg, wu, wd)):
        remote(src, w_part(i, c), w_send.at[i], w_recv.at[i], (x, sibling)).start()
        pltpu.make_async_copy(src, w_part(i, c), w_loc.at[i]).start()
    each(TOK // 16, blank)
    wait_bytes(meta.at[pl.ds(1, NZ - 1)], m_recv)
    each(chip_h // 16, clear)
    weights_here()

    def during(lo, t, f):
        @pl.when((t >= lo) & (t < lo + NCH))
        def _():
            f(t - lo)

    def step(t):
        @pl.when(t < 8)
        def _():
            relay_step(t // 4, lax.rem(t, 4) + 1)

        @pl.when(t == 2)
        def _():
            ring_send(1, 1, og_in)

        during(1, t, tok_chunk)
        during(2, t, up_gate_mid)
        during(3, t, act)
        during(4, t, hid_pass)
        during(5, t, expert_out)

        @pl.when(t == 9)
        def _():
            for g, rows in enumerate(BACK):
                give_back(*rows, g)

        during(8, t, cot_chunk)
        during(9, t, hidden_mid)
        during(10, t, grad_rows)
        during(9, t, down_step)
        during(11, t, grads_pass)
        during(12, t, gate_step)

        @pl.when(t == 13)
        def _():
            send_pair(2)

        @pl.when(t == 16)
        def _():
            send_pair(0)
            send_pair(1)

        def from_step(start, n):
            return jnp.where(t >= start, n, 0)

        done = from_step(14, 1) + from_step(16, 2) + from_step(18, 2) + from_step(20, 2)
        due = from_step(13, 1) + from_step(15, 2) + from_step(17, 2) + from_step(19, 2) + from_step(20, 1)
        lax.fori_loop(done, due, lambda n, carry: (fold(n), carry)[1], 0)

        @pl.when(t == 18)
        def _():
            join_pair(2, g_down)
            join_pair(0, g_gate)
            join_pair(1, g_up)

    each(21, step)
    mine = sum_s[...]

    for d in range(2):
        fold_wait(4, d)
        mine += ring_in[d, 3].astype(F32)
    out[...] = mine.astype(BF)

    for i in range(3):
        wait_bytes(wg, w_send.at[i])
        wait_bytes(pair_out.at[i], pair_send.at[i])
    wait_bytes(meta.at[pl.ds(1, NZ - 1)], m_send)
    for d in range(2):
        lanes = pl.ds(d * half_f, half_f)
        for k in range(1, 5):
            for a in range(2):
                wait_bytes(src_rows.at[a, 0] if k < 4 else src_rows.at[a, 0, :, lanes], z_send.at[a, d, k - 1])
            wait_bytes(ring_out.at[d, k - 1] if k > 1 else ring_out.at[d, 0, :, lanes], r_send.at[d, k - 1])
    for dy in range(1, NY):
        for a in range(2):
            wait_bytes(staged.at[a, dy, pl.ds(0, PER_Y)], y_send.at[a, dy - 1])
    for g, (first, count) in enumerate(BACK):
        wait_bytes(rows_back.at[pl.ds(1, NY - 1), pl.ds(0, count)], o_send.at[g])
    for i in range(NCH):
        for d in range(2):
            wait_bytes(mid.at[d, i], pm_send.at[d, i])
            wait_bytes(part_in.at[d, i], p_send.at[d, i])
            wait_bytes(hid.at[i, x], h_send.at[d, i])
            wait_bytes(mid_h.at[d, i], h2_send.at[d, i])
            wait_bytes(mid_h.at[d, i], hm_send.at[d, i])
            wait_bytes(part_h_in.at[d, i], ph_send.at[d, i])
            wait_bytes(grads_x.at[i, x], gx_send.at[d, i])
            wait_bytes(grads_x.at[i, x, 0], g2_send.at[d, i])


def finish_kernel(*refs):
    count = (len(refs) - 2) // 3
    results, outs, held = refs[:count], refs[count:2 * count], refs[2 * count:3 * count]
    sem_in, sem_out = refs[-2:]
    first = [pltpu.make_async_copy(results[i], held[i], sem_in.at[i]) for i in range(count)]
    last = [pltpu.make_async_copy(held[i], outs[i], sem_out.at[i]) for i in range(count)]
    for copy in first:
        copy.start()
    for i in range(count):
        first[i].wait()
        last[i].start()
    for copy in last:
        copy.wait()


def finish(results):
    anywhere = pl.BlockSpec(memory_space=pl.ANY)
    count = len(results)
    return pl.pallas_call(
        finish_kernel,
        out_shape=tuple(jax.ShapeDtypeStruct(r.shape, r.dtype) for r in results),
        in_specs=[anywhere] * count,
        out_specs=[anywhere] * count,
        scratch_shapes=[pltpu.VMEM(r.shape, r.dtype) for r in results]
        + [pltpu.SemaphoreType.DMA((count,)), pltpu.SemaphoreType.DMA((count,))],
    )(*results)


def run_layer(tokens, out_grad, ids, route, wg, wu, wd):
    own_h, feats = wg.shape
    qh = 2 * own_h // NX
    dma = pltpu.SemaphoreType.DMA
    vm = pltpu.VMEM
    scratch = [
        vm((3, 2 * own_h, feats), BF), vm((NZ + 1, 8, TOK), F32),
        vm((2, NZ + 1, TOK, feats), BF), vm((2, NCH, NY, GROUP, feats), BF),
        vm((2, NY, 4 * STEP - EARLY + STEP, feats), BF),
        vm((NY * STEP, 3 * TOK), BF), vm((NY * STEP, TOK), F32),
        vm((NX, NCH, 2, qh, CHUNK), BF), vm((2, NCH, 2, qh, CHUNK), BF), vm((2, NCH, qh, CHUNK), BF),
        vm((NCH, NX, qh, CHUNK), BF),
        vm((NX, NCH, qh, CHUNK), BF), vm((2, NCH, qh, CHUNK), BF), vm((2, NCH, qh, CHUNK // 2), BF),
        vm((NCH, NX, 2, qh, CHUNK), BF),
        vm((NCH, qh, CHUNK), F32), vm((NCH, qh, CHUNK), F32), vm((NCH, qh, CHUNK), F32),
        vm((NCH, NY - 1, GROUP, feats), BF), vm((NY, PER_Y, feats), BF),
        vm((2, NY * WINDOW, TOK), BF), vm((TOK, feats), F32),
        vm((2, 4, TOK, feats), BF), vm((2, 4, TOK, feats), BF),
        vm((3, 2 * own_h, feats), F32),
        vm((3, own_h, feats), BF), vm((3, own_h, feats), BF),
        dma((3,)), dma((3,)), dma((3,)), dma, dma, dma((2,)),
        dma((2, 2, 4)), dma((2, 2, 4)), dma((2, NY - 1)), dma((2, NCH)),
        *[dma((2, NCH))] * 16,
        dma((len(BACK),)), dma((len(BACK),)), dma((2, 4)), dma((2, 4)),
        dma((3,)), dma((3,)),
    ]
    anywhere = pl.BlockSpec(memory_space=pl.ANY)
    inside = pl.BlockSpec(memory_space=pltpu.VMEM)
    return pl.pallas_call(
        layer_kernel,
        out_shape=(
            jax.ShapeDtypeStruct((TOK, feats), BF),
            jax.ShapeDtypeStruct((own_h, feats), BF),
            jax.ShapeDtypeStruct((own_h, feats), BF),
            jax.ShapeDtypeStruct((own_h, feats), BF),
        ),
        in_specs=[anywhere] * 2 + [inside] * 2 + [anywhere] * 3,
        out_specs=[inside] * 4,
        scratch_shapes=scratch,
        compiler_params=pltpu.CompilerParams(
            collective_id=0, has_side_effects=True, vmem_limit_bytes=60 * 1024 * 1024),
    )(tokens, out_grad, ids, route, wg, wu, wd)


def per_device(tokens, expert_ids, route_weights, w_gate, w_up, w_down, out_grad):
    return finish(run_layer(
        tokens, out_grad, expert_ids.T, route_weights.T, w_gate, w_up, w_down))


def solution(mesh):
    placed = (
        P("expert", "dp"),
        P("expert", None),
        P("expert", None),
        P("expert", "dp"),
        P("expert", "dp"),
        P("expert", "dp"),
        P("expert", "dp"),
    )
    return jax.shard_map(
        per_device,
        mesh=mesh,
        in_specs=placed,
        out_specs=(P("expert", "dp"), P("expert", "dp"), P("expert", "dp"), P("expert", "dp")),
        check_vma=False,
    )
```

```python
import jax
import jax.numpy as jnp
from jax import lax
from jax.experimental import pallas as pl
from jax.experimental.pallas import tpu as pltpu
from jax.sharding import PartitionSpec as P

NX, NY, NZ = 4, 4, 8
SLICES = 8
SLOT = 40
CODE = 64
TOK = 128
PER_Y = NZ * SLOT
ROWS = NY * PER_Y
GROUP = 64
CHUNK = NY * GROUP
NCH = PER_Y // GROUP
WINDOW = 48
TILE = 256
STEP, EARLY = 80, 48
BACK = ((272, 48), (192, 80), (112, 80), (32, 80), (0, 32))
PLACE = (0, 1, 3, 5, 7, 6, 4, 2)
MESH = pl.DeviceIdType.MESH
BF = jnp.bfloat16
F32 = jnp.float32
CROSS_LAST = (((1,), (1,)), ((), ()))
CROSS_FIRST = (((0,), (0,)), ((), ()))
PLAIN = (((1,), (0,)), ((), ()))


def dot(a, b, dims):
    return lax.dot_general(a, b, dims, preferred_element_type=F32)


def layer_kernel(
    tok_in, og_in, ids, route, wg, wu, wd,
    out, g_gate, g_up, g_down,
    w, meta, src_rows, xc, staged, hit_s, scale_s,
    part, part_in, mid, hid, part_h, part_h_in, mid_h, grads_x,
    up_s, act_s, slope_s, rows_out, rows_back,
    back_w, sum_s, ring_out, ring_in, acc, pair_out, pair_in,
    w_loc, w_send, w_recv, m_send, m_recv, own_sem,
    z_send, z_recv, y_send, y_recv,
    pm_send, pm_recv, p_send, p_recv, h_send, h_recv, h2_send, h2_recv,
    hm_send, hm_recv, ph_send, ph_recv, gx_send, gx_recv, g2_send, g2_recv,
    o_send, o_recv, r_send, r_recv, pair_send, pair_recv,
):
    own_h, feats = wg.shape
    half_f = feats // 2
    chip_h = 2 * own_h
    quarter_h = chip_h // NX
    x = lax.axis_index("dp")
    e = lax.axis_index("expert")
    c = lax.rem(e, 2)
    chip = e // 2
    z = lax.rem(chip, NZ)
    y = chip // NZ
    half = z // 4
    sibling = e + 1 - 2 * c

    def chip_at(dy, dz):
        return (x, (lax.rem(y + dy, NY) * NZ + lax.rem(z + dz, NZ)) * 2 + c)

    def x_peer(k):
        return lax.rem(x + k, NX)

    def remote(src, dst, send_sem, recv_sem, dev):
        return pltpu.make_async_remote_copy(
            src_ref=src, dst_ref=dst, send_sem=send_sem, recv_sem=recv_sem,
            device_id=dev, device_id_type=MESH)

    def wait_bytes(ref, sem):
        pltpu.make_async_copy(ref, ref, sem).wait()

    def set_meta():
        slices = lax.div(ids[...], 8)
        number = lax.broadcasted_iota(jnp.int32, (SLICES, TOK), 0)
        hit0 = (slices[0:1] == number).astype(F32)
        hit1 = (slices[1:2] == number).astype(F32)
        earlier = (lax.broadcasted_iota(jnp.int32, (TOK, TOK), 0)
                   < lax.broadcasted_iota(jnp.int32, (TOK, TOK), 1)).astype(F32).astype(BF)
        before = dot((hit0 + hit1).astype(BF), earlier, PLAIN)
        code = slices.astype(F32) * float(CODE)
        meta[0, 0:1] = code[0:1] + jnp.sum(hit0 * before, axis=0, keepdims=True)
        meta[0, 1:2] = code[1:2] + jnp.sum(hit1 * (before + hit0), axis=0, keepdims=True)
        meta[0, 2:4] = route[...]
        meta[0, 4:8] = jnp.zeros((4, TOK), F32)
        meta[NZ] = jnp.full((8, TOK), -1.0, F32)

    def each(count, f):
        lax.fori_loop(0, count, lambda i, carry: (f(i), carry)[1], 0)

    def blank(row):
        for a in range(2):
            src_rows[a, NZ, pl.ds(pl.multiple_of(row * 16, 16), 16)] = jnp.zeros((16, feats), BF)
            ring_in[a, 0, pl.ds(pl.multiple_of(row * 16, 16), 16), (1 - a) * half_f:(2 - a) * half_f] = (
                jnp.zeros((16, half_f), BF))

    def clear(row):
        for kind in range(3):
            acc[kind, pl.ds(pl.multiple_of(row * 16, 16), 16)] = jnp.zeros((16, feats), F32)

    def weights(dy, place, first, count):
        codes = meta[place, 0:2, :] - ((lax.rem(y + dy, NY) * 2 + half) * CODE).astype(F32)
        start = jnp.asarray(place * SLOT, jnp.int32).astype(F32)
        at = jnp.where((codes >= 0.0) & (codes < float(SLOT)), codes + start, -1.0)
        row = (lax.broadcasted_iota(jnp.int32, (count, TOK), 0) + first).astype(F32)
        return (jnp.where(row == at[0:1], meta[place, 2:3, :], 0.0)
                + jnp.where(row == at[1:2], meta[place, 3:4, :], 0.0))

    def spans(first, count):
        found, row = [], first
        while row < first + count:
            i = row // GROUP
            n = min(first + count, (i + 1) * GROUP) - row
            found.append((i, row - i * GROUP, row, n))
            row += n
        return found

    def choose(a, first, count, place, places):
        def one_y(dy):
            wts = jnp.concatenate([weights(dy, place + n, first, count) for n in range(places)], axis=1)
            here = pl.ds(pl.multiple_of(dy * count, 16), count)
            hit_s[here, 0:places * TOK] = (wts > 0.0).astype(F32).astype(BF)
            total = jnp.sum(wts, axis=1, keepdims=True)
            scale_s[here] = jnp.broadcast_to(jnp.where(a == 1, total, jnp.ones_like(total)), (count, TOK))

        def tile(n):
            lanes = pl.ds(pl.multiple_of(n * TILE, TILE), TILE)
            rows = src_rows[a, pl.ds(place, places), :, lanes].reshape(places * TOK, TILE)
            picked = dot(hit_s[0:NY * count, 0:places * TOK], rows, PLAIN)
            picked = (scale_s[0:NY * count, 0:1] * picked).astype(BF)
            for dy in range(NY):
                staged[a, dy, pl.ds(pl.multiple_of(first, 16), count), lanes] = picked[dy * count:(dy + 1) * count]

        each(NY, one_y)
        each(feats // TILE, tile)

    barrier = pltpu.get_barrier_semaphore()
    friends = [chip_at(0, d) for d in range(1, NZ)] + [chip_at(d, 0) for d in range(1, NY)]
    friends += [(x_peer(k), e) for k in range(1, NX)] + [(x, sibling)]
    for dev in friends:
        pl.semaphore_signal(barrier, inc=1, device_id=dev, device_id_type=MESH)
    pltpu.make_async_copy(tok_in, src_rows.at[0, 0], own_sem.at[0]).start()
    pltpu.make_async_copy(og_in, src_rows.at[1, 0], own_sem.at[1]).start()
    set_meta()
    for a in range(2):
        wait_bytes(src_rows.at[a, 0], own_sem.at[a])
    each(2, lambda a: choose(a, 0, 32, 0, 1))
    pl.semaphore_wait(barrier, len(friends))

    def ring_send(a, k, own=None):
        for d in range(2):
            if k == 1:
                src, dst = own, src_rows.at[a, 1 + d]
            else:
                src, dst = src_rows.at[a, 2 * k - 3 + d], src_rows.at[a, 2 * k - 1 + d if k < 4 else 7]
            if k == 4:
                lanes = pl.ds(d * half_f, half_f)
                src, dst = src.at[:, lanes], dst.at[:, lanes]
            remote(src, dst, z_send.at[a, d, k - 1], z_recv.at[a, d, k - 1],
                   chip_at(0, 1 if d == 0 else NZ - 1)).start()

    def ring_wait(a, k):
        for d in range(2):
            ref = src_rows.at[a, 2 * k - 1 + d] if k < 4 else src_rows.at[a, 7, :, pl.ds(d * half_f, half_f)]
            wait_bytes(ref, z_recv.at[a, d, k - 1])

    ring_send(0, 1, tok_in)
    for d in range(1, NZ):
        remote(meta.at[0], meta.at[PLACE[d]], m_send, m_recv, chip_at(0, d)).start()

    def w_part(i, core):
        return w.at[i, pl.ds(pl.multiple_of(core * own_h, 16), own_h)]

    def pass_on(a, first, count):
        for dy in (1, 3, 2):
            for i, off, row, n in spans(first, count):
                remote(staged.at[a, dy, pl.ds(row, n)], xc.at[a, i, dy, pl.ds(off, n)],
                       y_send.at[a, dy - 1], y_recv.at[a, i], chip_at(dy, 0)).start()
        for i, off, row, n in spans(first, count):
            pltpu.make_async_copy(staged.at[a, 0, pl.ds(row, n)], xc.at[a, i, 0, pl.ds(off, n)],
                                  y_recv.at[a, i]).start()

    def relay_step(a, k):
        for j in range(1, 5):
            @pl.when(k == j)
            def _(j=j):
                ring_wait(a, j)
                if j < 4:
                    ring_send(a, j + 1)
        choose(a, STEP * k - EARLY, STEP, 2 * k - 2, 3)
        for j in range(1, 5):
            @pl.when(k == j)
            def _(j=j):
                pass_on(a, STEP * j - EARLY, min(STEP, PER_Y - STEP * j + EARLY))

    left, far, right = x_peer(NX - 1), x_peer(2), x_peer(1)
    near_half, far_half = pl.ds(0, CHUNK // 2), pl.ds(CHUNK // 2, CHUNK // 2)

    def both_sides(rightward, leftward, send, recv, i):
        for d, (src, dst) in enumerate((rightward, leftward)):
            remote(src, dst, send.at[d, i], recv.at[d, i], ((right, left)[d], e)).start()

    def add_to(ref, extra):
        ref[...] = (ref[...].astype(F32) + extra.astype(F32)).astype(BF)

    def chunk(ref, i):
        return xc[ref, i].reshape(CHUNK, feats)

    def up_gate(i):
        rows = chunk(0, i)

        def one(kind):
            prod = dot(w[kind], rows, CROSS_LAST).astype(BF)
            for q in range(NX):
                part[q, i, kind] = prod[q * quarter_h:(q + 1) * quarter_h]

        each(2, one)
        both_sides((part.at[far, i, 0], mid.at[0, i]), (part.at[far, i, 1], mid.at[1, i]), pm_send, pm_recv, i)

    def up_gate_mid(i):
        wait_bytes(mid.at[0, i], pm_recv.at[0, i])
        wait_bytes(mid.at[1, i], pm_recv.at[1, i])
        add_to(part.at[right, i, 0], mid[0, i])
        add_to(part.at[left, i, 1], mid[1, i])
        both_sides((part.at[right, i], part_in.at[0, i]), (part.at[left, i], part_in.at[1, i]), p_send, p_recv, i)

    def act(i):
        for d in range(2):
            wait_bytes(part_in.at[d, i], p_recv.at[d, i])
        gate = part[x, i, 0].astype(F32)
        up = part[x, i, 1].astype(F32)
        for d in range(2):
            gate += part_in[d, i, 0].astype(F32)
            up += part_in[d, i, 1].astype(F32)
        sig = jax.nn.sigmoid(gate)
        active = gate * sig
        up_s[i] = up
        act_s[i] = active
        slope_s[i] = sig * (1.0 + gate * (1.0 - sig))
        hid[i, x] = (active * up).astype(BF)
        both_sides((hid.at[i, x], hid.at[i, x]), (hid.at[i, x], hid.at[i, x]), h_send, h_recv, i)

    def hid_pass(i):
        wait_bytes(hid.at[i, left], h_recv.at[0, i])
        wait_bytes(hid.at[i, right], h_recv.at[1, i])
        both_sides((hid.at[i, left, :, near_half],) * 2, (hid.at[i, right, :, far_half],) * 2, h2_send, h2_recv, i)

    def expert_out(i):
        wait_bytes(hid.at[i, far, :, near_half], h2_recv.at[0, i])
        wait_bytes(hid.at[i, far, :, far_half], h2_recv.at[1, i])
        prod = dot(hid[i].reshape(chip_h, CHUNK), w[2], CROSS_FIRST).astype(BF)
        rows_back[0, pl.ds(pl.multiple_of(i * GROUP, GROUP), GROUP)] = prod[0:GROUP]
        for dy in range(1, NY):
            rows_out[i, dy - 1] = prod[dy * GROUP:(dy + 1) * GROUP]

    def hidden_part(i):
        prod = dot(w[2], chunk(1, i), CROSS_LAST).astype(BF)
        for q in range(NX):
            part_h[q, i] = prod[q * quarter_h:(q + 1) * quarter_h]
        both_sides((part_h.at[far, i, :, near_half], mid_h.at[0, i]),
                   (part_h.at[far, i, :, far_half], mid_h.at[1, i]), hm_send, hm_recv, i)

    def hidden_mid(i):
        wait_bytes(mid_h.at[0, i], hm_recv.at[0, i])
        wait_bytes(mid_h.at[1, i], hm_recv.at[1, i])
        add_to(part_h.at[right, i, :, near_half], mid_h[0, i])
        add_to(part_h.at[left, i, :, far_half], mid_h[1, i])
        both_sides((part_h.at[right, i], part_h_in.at[0, i]), (part_h.at[left, i], part_h_in.at[1, i]),
                   ph_send, ph_recv, i)

    def grad_rows(i):
        for d in range(2):
            wait_bytes(part_h_in.at[d, i], ph_recv.at[d, i])
        gh = part_h[x, i].astype(F32)
        for d in range(2):
            gh += part_h_in[d, i].astype(F32)
        grads_x[i, x, 0] = (gh * up_s[i] * slope_s[i]).astype(BF)
        grads_x[i, x, 1] = (gh * act_s[i]).astype(BF)
        both_sides((grads_x.at[i, x],) * 2, (grads_x.at[i, x],) * 2, gx_send, gx_recv, i)

    def grads_pass(i):
        wait_bytes(grads_x.at[i, left], gx_recv.at[0, i])
        wait_bytes(grads_x.at[i, right], gx_recv.at[1, i])
        both_sides((grads_x.at[i, left, 0],) * 2, (grads_x.at[i, right, 1],) * 2, g2_send, g2_recv, i)

    def down_step(i):
        acc[2] += dot(hid[i].reshape(chip_h, CHUNK), chunk(1, i), PLAIN)

    def gate_step(i):
        wait_bytes(grads_x.at[i, far, 0], g2_recv.at[0, i])
        wait_bytes(grads_x.at[i, far, 1], g2_recv.at[1, i])

        def one(kind):
            acc[kind] += dot(grads_x[i, :, kind].reshape(chip_h, CHUNK), chunk(0, i), PLAIN)

        each(2, one)

    def give_back(first, count, g):
        for dy in (1, 3, 2):
            for i, off, row, n in spans(first, count):
                remote(rows_out.at[i, dy - 1, pl.ds(off, n)], rows_back.at[dy, pl.ds(row, n)],
                       o_send.at[g], o_recv.at[g], chip_at(NY - dy, 0)).start()

    def await_back(g):
        first, count = BACK[g]
        wait_bytes(rows_back.at[pl.ds(1, NY - 1), pl.ds(first, count)], o_recv.at[g])

    def dense(place):
        first = pl.multiple_of(place * SLOT // 16 * 16, 16)

        def one_y(dy):
            wts = weights(dy, place, first, WINDOW)
            coarse = wts.astype(BF)
            here = pl.ds(pl.multiple_of(dy * WINDOW, 16), WINDOW)
            back_w[0, here] = coarse
            back_w[1, here] = (wts - coarse.astype(F32)).astype(BF)

        def tile(n):
            lanes = pl.ds(pl.multiple_of(n * TILE, TILE), TILE)
            rows = rows_back[:, pl.ds(first, WINDOW), lanes].reshape(NY * WINDOW, TILE)
            sum_s[:, lanes] = dot(back_w[0], rows, CROSS_FIRST) + dot(back_w[1], rows, CROSS_FIRST)

        each(NY, one_y)
        each(feats // TILE, tile)

    def fold_send(k, d):
        src, dst = ring_out.at[d, k - 1], ring_in.at[d, k - 1]
        if k == 1:
            lanes = pl.ds(d * half_f, half_f)
            src, dst = src.at[:, lanes], dst.at[:, lanes]
        remote(src, dst, r_send.at[d, k - 1], r_recv.at[d, k - 1], chip_at(0, 1 if d == 0 else NZ - 1)).start()

    def fold_wait(k, d):
        ref = ring_in.at[d, k - 1]
        wait_bytes(ref.at[:, pl.ds(d * half_f, half_f)] if k == 1 else ref, r_recv.at[d, k - 1])

    def fold(n):
        for j, groups in ((0, (0,)), (1, (1,)), (3, (2,)), (5, (3,)), (7, (4,))):
            @pl.when(n == j)
            def _(groups=groups):
                for g in groups:
                    await_back(g)
        dense(7 - n)

        @pl.when(n == 0)
        def _():
            for d in range(2):
                ring_out[d, 0] = sum_s[...].astype(BF)
                fold_send(1, d)

        for j in range(1, 7):
            @pl.when(n == j)
            def _(k=(j + 3) // 2, d=(j - 1) % 2):
                fold_wait(k - 1, d)

        @pl.when((n >= 1) & (n <= 6))
        def _():
            k = (n + 3) // 2
            d = lax.rem(n - 1, 2)
            ring_out[d, k - 1] = (sum_s[...] + ring_in[d, k - 2].astype(F32)).astype(BF)

        for j in range(1, 7):
            @pl.when(n == j)
            def _(k=(j + 3) // 2, d=(j - 1) % 2):
                fold_send(k, d)

    def send_pair(kind):
        pair_out[kind] = acc[kind, pl.ds(pl.multiple_of((1 - c) * own_h, 16), own_h)].astype(BF)
        remote(pair_out.at[kind], pair_in.at[kind], pair_send.at[kind], pair_recv.at[kind],
               (x, sibling)).start()

    def join_pair(kind, dest):
        wait_bytes(pair_in.at[kind], pair_recv.at[kind])
        dest[...] = (acc[kind, pl.ds(pl.multiple_of(c * own_h, 16), own_h)]
                     + pair_in[kind].astype(F32)).astype(BF)

    def tok_chunk(i):
        wait_bytes(xc.at[0, i], y_recv.at[0, i])
        up_gate(i)

    def cot_chunk(i):
        wait_bytes(xc.at[1, i], y_recv.at[1, i])
        hidden_part(i)

    def weights_here():
        for i, src in enumerate((wg, wu, wd)):
            wait_bytes(w_part(i, c), w_loc.at[i])
            wait_bytes(w_part(i, 1 - c), w_recv.at[i])

    for a in range(2):
        pass_on(a, 0, 32)
    for i, src in enumerate((wg, wu, wd)):
        remote(src, w_part(i, c), w_send.at[i], w_recv.at[i], (x, sibling)).start()
        pltpu.make_async_copy(src, w_part(i, c), w_loc.at[i]).start()
    each(TOK // 16, blank)
    wait_bytes(meta.at[pl.ds(1, NZ - 1)], m_recv)
    each(chip_h // 16, clear)
    weights_here()

    def during(lo, t, f):
        @pl.when((t >= lo) & (t < lo + NCH))
        def _():
            f(t - lo)

    def step(t):
        @pl.when(t < 8)
        def _():
            relay_step(t // 4, lax.rem(t, 4) + 1)

        @pl.when(t == 2)
        def _():
            ring_send(1, 1, og_in)

        during(1, t, tok_chunk)
        during(2, t, up_gate_mid)
        during(3, t, act)
        during(4, t, hid_pass)
        during(5, t, expert_out)

        @pl.when(t == 9)
        def _():
            for g, rows in enumerate(BACK):
                give_back(*rows, g)

        during(7, t, cot_chunk)
        during(8, t, hidden_mid)
        during(9, t, grad_rows)
        during(9, t, down_step)
        during(10, t, grads_pass)
        during(11, t, gate_step)

        @pl.when(t == 13)
        def _():
            send_pair(2)

        @pl.when(t == 15)
        def _():
            send_pair(0)
            send_pair(1)

        def from_step(start, n):
            return jnp.where(t >= start, n, 0)

        done = from_step(11, 1) + from_step(12, 2) + from_step(14, 2) + from_step(15, 2) + from_step(17, 1)
        due = from_step(10, 1) + from_step(11, 2) + from_step(13, 2) + from_step(14, 2) + from_step(16, 1)
        lax.fori_loop(done, due, lambda n, carry: (fold(n), carry)[1], 0)

        @pl.when(t == 16)
        def _():
            join_pair(2, g_down)
            join_pair(0, g_gate)
            join_pair(1, g_up)

    each(17, step)
    mine = sum_s[...]

    for d in range(2):
        fold_wait(4, d)
        mine += ring_in[d, 3].astype(F32)
    out[...] = mine.astype(BF)

    for i in range(3):
        wait_bytes(wg, w_send.at[i])
        wait_bytes(pair_out.at[i], pair_send.at[i])
    wait_bytes(meta.at[pl.ds(1, NZ - 1)], m_send)
    for d in range(2):
        lanes = pl.ds(d * half_f, half_f)
        for k in range(1, 5):
            for a in range(2):
                wait_bytes(src_rows.at[a, 0] if k < 4 else src_rows.at[a, 0, :, lanes], z_send.at[a, d, k - 1])
            wait_bytes(ring_out.at[d, k - 1] if k > 1 else ring_out.at[d, 0, :, lanes], r_send.at[d, k - 1])
    for dy in range(1, NY):
        for a in range(2):
            wait_bytes(staged.at[a, dy, pl.ds(0, PER_Y)], y_send.at[a, dy - 1])
    for g, (first, count) in enumerate(BACK):
        wait_bytes(rows_back.at[pl.ds(1, NY - 1), pl.ds(0, count)], o_send.at[g])
    for i in range(NCH):
        for d in range(2):
            wait_bytes(mid.at[d, i], pm_send.at[d, i])
            wait_bytes(part_in.at[d, i], p_send.at[d, i])
            wait_bytes(hid.at[i, x], h_send.at[d, i])
            wait_bytes(mid_h.at[d, i], h2_send.at[d, i])
            wait_bytes(mid_h.at[d, i], hm_send.at[d, i])
            wait_bytes(part_h_in.at[d, i], ph_send.at[d, i])
            wait_bytes(grads_x.at[i, x], gx_send.at[d, i])
            wait_bytes(grads_x.at[i, x, 0], g2_send.at[d, i])


def finish_kernel(*refs):
    count = (len(refs) - 2) // 3
    results, outs, held = refs[:count], refs[count:2 * count], refs[2 * count:3 * count]
    sem_in, sem_out = refs[-2:]
    first = [pltpu.make_async_copy(results[i], held[i], sem_in.at[i]) for i in range(count)]
    last = [pltpu.make_async_copy(held[i], outs[i], sem_out.at[i]) for i in range(count)]
    for copy in first:
        copy.start()
    for i in range(count):
        first[i].wait()
        last[i].start()
    for copy in last:
        copy.wait()


def finish(results):
    anywhere = pl.BlockSpec(memory_space=pl.ANY)
    count = len(results)
    return pl.pallas_call(
        finish_kernel,
        out_shape=tuple(jax.ShapeDtypeStruct(r.shape, r.dtype) for r in results),
        in_specs=[anywhere] * count,
        out_specs=[anywhere] * count,
        scratch_shapes=[pltpu.VMEM(r.shape, r.dtype) for r in results]
        + [pltpu.SemaphoreType.DMA((count,)), pltpu.SemaphoreType.DMA((count,))],
    )(*results)


def run_layer(tokens, out_grad, ids, route, wg, wu, wd):
    own_h, feats = wg.shape
    qh = 2 * own_h // NX
    dma = pltpu.SemaphoreType.DMA
    vm = pltpu.VMEM
    scratch = [
        vm((3, 2 * own_h, feats), BF), vm((NZ + 1, 8, TOK), F32),
        vm((2, NZ + 1, TOK, feats), BF), vm((2, NCH, NY, GROUP, feats), BF),
        vm((2, NY, 4 * STEP - EARLY + STEP, feats), BF),
        vm((NY * STEP, 3 * TOK), BF), vm((NY * STEP, TOK), F32),
        vm((NX, NCH, 2, qh, CHUNK), BF), vm((2, NCH, 2, qh, CHUNK), BF), vm((2, NCH, qh, CHUNK), BF),
        vm((NCH, NX, qh, CHUNK), BF),
        vm((NX, NCH, qh, CHUNK), BF), vm((2, NCH, qh, CHUNK), BF), vm((2, NCH, qh, CHUNK // 2), BF),
        vm((NCH, NX, 2, qh, CHUNK), BF),
        vm((NCH, qh, CHUNK), F32), vm((NCH, qh, CHUNK), F32), vm((NCH, qh, CHUNK), F32),
        vm((NCH, NY - 1, GROUP, feats), BF), vm((NY, PER_Y, feats), BF),
        vm((2, NY * WINDOW, TOK), BF), vm((TOK, feats), F32),
        vm((2, 4, TOK, feats), BF), vm((2, 4, TOK, feats), BF),
        vm((3, 2 * own_h, feats), F32),
        vm((3, own_h, feats), BF), vm((3, own_h, feats), BF),
        dma((3,)), dma((3,)), dma((3,)), dma, dma, dma((2,)),
        dma((2, 2, 4)), dma((2, 2, 4)), dma((2, NY - 1)), dma((2, NCH)),
        *[dma((2, NCH))] * 16,
        dma((len(BACK),)), dma((len(BACK),)), dma((2, 4)), dma((2, 4)),
        dma((3,)), dma((3,)),
    ]
    anywhere = pl.BlockSpec(memory_space=pl.ANY)
    inside = pl.BlockSpec(memory_space=pltpu.VMEM)
    return pl.pallas_call(
        layer_kernel,
        out_shape=(
            jax.ShapeDtypeStruct((TOK, feats), BF),
            jax.ShapeDtypeStruct((own_h, feats), BF),
            jax.ShapeDtypeStruct((own_h, feats), BF),
            jax.ShapeDtypeStruct((own_h, feats), BF),
        ),
        in_specs=[anywhere] * 2 + [inside] * 2 + [anywhere] * 3,
        out_specs=[inside] * 4,
        scratch_shapes=scratch,
        compiler_params=pltpu.CompilerParams(
            collective_id=0, has_side_effects=True, vmem_limit_bytes=60 * 1024 * 1024),
    )(tokens, out_grad, ids, route, wg, wu, wd)


def per_device(tokens, expert_ids, route_weights, w_gate, w_up, w_down, out_grad):
    return finish(run_layer(
        tokens, out_grad, expert_ids.T, route_weights.T, w_gate, w_up, w_down))


def solution(mesh):
    placed = (
        P("expert", "dp"),
        P("expert", None),
        P("expert", None),
        P("expert", "dp"),
        P("expert", "dp"),
        P("expert", "dp"),
        P("expert", "dp"),
    )
    return jax.shard_map(
        per_device,
        mesh=mesh,
        in_specs=placed,
        out_specs=(P("expert", "dp"), P("expert", "dp"), P("expert", "dp"), P("expert", "dp")),
        check_vma=False,
    )
```

```python
import jax
import jax.numpy as jnp
from jax import lax
from jax.experimental import pallas as pl
from jax.experimental.pallas import tpu as pltpu
from jax.sharding import PartitionSpec as P

NX, NY, NZ = 4, 4, 8
SLICES = 8
SLOT = 40
CODE = 64
TOK = 128
PER_Y = NZ * SLOT
ROWS = NY * PER_Y
GROUP = 64
CHUNK = NY * GROUP
NCH = PER_Y // GROUP
WINDOW = 48
TILE = 256
STEP, EARLY = 80, 48
BACK = ((272, 48), (192, 80), (112, 80), (32, 80), (0, 32))
PLACE = (0, 1, 3, 5, 7, 6, 4, 2)
MESH = pl.DeviceIdType.MESH
BF = jnp.bfloat16
F32 = jnp.float32
CROSS_LAST = (((1,), (1,)), ((), ()))
CROSS_FIRST = (((0,), (0,)), ((), ()))
PLAIN = (((1,), (0,)), ((), ()))


def dot(a, b, dims):
    return lax.dot_general(a, b, dims, preferred_element_type=F32)


def layer_kernel(
    tok_in, og_in, ids, route, wg, wu, wd,
    out, g_gate, g_up, g_down,
    w, meta, src_rows, xc, staged, hit_s, scale_s,
    part, part_in, mid, hid, part_h, part_h_in, mid_h, grads_x,
    up_s, act_s, slope_s, rows_out, rows_back,
    back_w, sum_s, ring_out, ring_in, acc, pair_out, pair_in,
    w_loc, w_send, w_recv, m_send, m_recv, own_sem,
    z_send, z_recv, y_send, y_recv,
    pm_send, pm_recv, p_send, p_recv, h_send, h_recv, h2_send, h2_recv,
    hm_send, hm_recv, ph_send, ph_recv, gx_send, gx_recv, g2_send, g2_recv,
    o_send, o_recv, r_send, r_recv, pair_send, pair_recv,
):
    own_h, feats = wg.shape
    half_f = feats // 2
    chip_h = 2 * own_h
    quarter_h = chip_h // NX
    x = lax.axis_index("dp")
    e = lax.axis_index("expert")
    c = lax.rem(e, 2)
    chip = e // 2
    z = lax.rem(chip, NZ)
    y = chip // NZ
    half = z // 4
    sibling = e + 1 - 2 * c

    def chip_at(dy, dz):
        return (x, (lax.rem(y + dy, NY) * NZ + lax.rem(z + dz, NZ)) * 2 + c)

    def x_peer(k):
        return lax.rem(x + k, NX)

    def remote(src, dst, send_sem, recv_sem, dev):
        return pltpu.make_async_remote_copy(
            src_ref=src, dst_ref=dst, send_sem=send_sem, recv_sem=recv_sem,
            device_id=dev, device_id_type=MESH)

    def wait_bytes(ref, sem):
        pltpu.make_async_copy(ref, ref, sem).wait()

    def set_meta():
        slices = lax.div(ids[...], 8)
        number = lax.broadcasted_iota(jnp.int32, (SLICES, TOK), 0)
        hit0 = (slices[0:1] == number).astype(F32)
        hit1 = (slices[1:2] == number).astype(F32)
        earlier = (lax.broadcasted_iota(jnp.int32, (TOK, TOK), 0)
                   < lax.broadcasted_iota(jnp.int32, (TOK, TOK), 1)).astype(F32).astype(BF)
        before = dot((hit0 + hit1).astype(BF), earlier, PLAIN)
        code = slices.astype(F32) * float(CODE)
        meta[0, 0:1] = code[0:1] + jnp.sum(hit0 * before, axis=0, keepdims=True)
        meta[0, 1:2] = code[1:2] + jnp.sum(hit1 * (before + hit0), axis=0, keepdims=True)
        meta[0, 2:4] = route[...]
        meta[0, 4:8] = jnp.zeros((4, TOK), F32)
        meta[NZ] = jnp.full((8, TOK), -1.0, F32)

    def each(count, f):
        lax.fori_loop(0, count, lambda i, carry: (f(i), carry)[1], 0)

    def blank(row):
        for a in range(2):
            src_rows[a, NZ, pl.ds(pl.multiple_of(row * 16, 16), 16)] = jnp.zeros((16, feats), BF)
            ring_in[a, 0, pl.ds(pl.multiple_of(row * 16, 16), 16), (1 - a) * half_f:(2 - a) * half_f] = (
                jnp.zeros((16, half_f), BF))

    def clear(row):
        for kind in range(3):
            acc[kind, pl.ds(pl.multiple_of(row * 16, 16), 16)] = jnp.zeros((16, feats), F32)

    def weights(dy, place, first, count):
        codes = meta[place, 0:2, :] - ((lax.rem(y + dy, NY) * 2 + half) * CODE).astype(F32)
        start = jnp.asarray(place * SLOT, jnp.int32).astype(F32)
        at = jnp.where((codes >= 0.0) & (codes < float(SLOT)), codes + start, -1.0)
        row = (lax.broadcasted_iota(jnp.int32, (count, TOK), 0) + first).astype(F32)
        return (jnp.where(row == at[0:1], meta[place, 2:3, :], 0.0)
                + jnp.where(row == at[1:2], meta[place, 3:4, :], 0.0))

    def spans(first, count):
        found, row = [], first
        while row < first + count:
            i = row // GROUP
            n = min(first + count, (i + 1) * GROUP) - row
            found.append((i, row - i * GROUP, row, n))
            row += n
        return found

    def choose(a, first, count, place, places):
        def one_y(dy):
            wts = jnp.concatenate([weights(dy, place + n, first, count) for n in range(places)], axis=1)
            here = pl.ds(pl.multiple_of(dy * count, 16), count)
            hit_s[here, 0:places * TOK] = (wts > 0.0).astype(F32).astype(BF)
            total = jnp.sum(wts, axis=1, keepdims=True)
            scale_s[here] = jnp.broadcast_to(jnp.where(a == 1, total, jnp.ones_like(total)), (count, TOK))

        def tile(n):
            lanes = pl.ds(pl.multiple_of(n * TILE, TILE), TILE)
            rows = src_rows[a, pl.ds(place, places), :, lanes].reshape(places * TOK, TILE)
            picked = dot(hit_s[0:NY * count, 0:places * TOK], rows, PLAIN)
            picked = (scale_s[0:NY * count, 0:1] * picked).astype(BF)
            for dy in range(NY):
                staged[a, dy, pl.ds(pl.multiple_of(first, 16), count), lanes] = picked[dy * count:(dy + 1) * count]

        each(NY, one_y)
        each(feats // TILE, tile)

    barrier = pltpu.get_barrier_semaphore()
    friends = [chip_at(0, d) for d in range(1, NZ)] + [chip_at(d, 0) for d in range(1, NY)]
    friends += [(x_peer(k), e) for k in range(1, NX)] + [(x, sibling)]
    for dev in friends:
        pl.semaphore_signal(barrier, inc=1, device_id=dev, device_id_type=MESH)
    pltpu.make_async_copy(tok_in, src_rows.at[0, 0], own_sem.at[0]).start()
    pltpu.make_async_copy(og_in, src_rows.at[1, 0], own_sem.at[1]).start()
    set_meta()
    for a in range(2):
        wait_bytes(src_rows.at[a, 0], own_sem.at[a])
    each(2, lambda a: choose(a, 0, 32, 0, 1))
    pl.semaphore_wait(barrier, len(friends))

    def ring_send(a, k, own=None):
        for d in range(2):
            if k == 1:
                src, dst = own, src_rows.at[a, 1 + d]
            else:
                src, dst = src_rows.at[a, 2 * k - 3 + d], src_rows.at[a, 2 * k - 1 + d if k < 4 else 7]
            if k == 4:
                lanes = pl.ds(d * half_f, half_f)
                src, dst = src.at[:, lanes], dst.at[:, lanes]
            remote(src, dst, z_send.at[a, d, k - 1], z_recv.at[a, d, k - 1],
                   chip_at(0, 1 if d == 0 else NZ - 1)).start()

    def ring_wait(a, k):
        for d in range(2):
            ref = src_rows.at[a, 2 * k - 1 + d] if k < 4 else src_rows.at[a, 7, :, pl.ds(d * half_f, half_f)]
            wait_bytes(ref, z_recv.at[a, d, k - 1])

    ring_send(0, 1, tok_in)
    for d in range(1, NZ):
        remote(meta.at[0], meta.at[PLACE[d]], m_send, m_recv, chip_at(0, d)).start()

    def w_part(i, core):
        return w.at[i, pl.ds(pl.multiple_of(core * own_h, 16), own_h)]

    def pass_on(a, first, count):
        for dy in (1, 3, 2):
            for i, off, row, n in spans(first, count):
                remote(staged.at[a, dy, pl.ds(row, n)], xc.at[a, i, dy, pl.ds(off, n)],
                       y_send.at[a, dy - 1], y_recv.at[a, i], chip_at(dy, 0)).start()
        for i, off, row, n in spans(first, count):
            pltpu.make_async_copy(staged.at[a, 0, pl.ds(row, n)], xc.at[a, i, 0, pl.ds(off, n)],
                                  y_recv.at[a, i]).start()

    def relay_step(a, k):
        for j in range(1, 5):
            @pl.when(k == j)
            def _(j=j):
                ring_wait(a, j)
                if j < 4:
                    ring_send(a, j + 1)
        choose(a, STEP * k - EARLY, STEP, 2 * k - 2, 3)
        for j in range(1, 5):
            @pl.when(k == j)
            def _(j=j):
                pass_on(a, STEP * j - EARLY, min(STEP, PER_Y - STEP * j + EARLY))

    left, far, right = x_peer(NX - 1), x_peer(2), x_peer(1)
    near_half, far_half = pl.ds(0, CHUNK // 2), pl.ds(CHUNK // 2, CHUNK // 2)

    def both_sides(rightward, leftward, send, recv, i):
        for d, (src, dst) in enumerate((rightward, leftward)):
            remote(src, dst, send.at[d, i], recv.at[d, i], ((right, left)[d], e)).start()

    def add_to(ref, extra):
        ref[...] = (ref[...].astype(F32) + extra.astype(F32)).astype(BF)

    def chunk(ref, i):
        return xc[ref, i].reshape(CHUNK, feats)

    def up_gate(i):
        rows = chunk(0, i)

        def one(kind):
            prod = dot(w[kind], rows, CROSS_LAST).astype(BF)
            for q in range(NX):
                part[q, i, kind] = prod[q * quarter_h:(q + 1) * quarter_h]

        each(2, one)
        both_sides((part.at[far, i, 0], mid.at[0, i]), (part.at[far, i, 1], mid.at[1, i]), pm_send, pm_recv, i)

    def up_gate_mid(i):
        wait_bytes(mid.at[0, i], pm_recv.at[0, i])
        wait_bytes(mid.at[1, i], pm_recv.at[1, i])
        add_to(part.at[right, i, 0], mid[0, i])
        add_to(part.at[left, i, 1], mid[1, i])
        both_sides((part.at[right, i], part_in.at[0, i]), (part.at[left, i], part_in.at[1, i]), p_send, p_recv, i)

    def act(i):
        for d in range(2):
            wait_bytes(part_in.at[d, i], p_recv.at[d, i])
        gate = part[x, i, 0].astype(F32)
        up = part[x, i, 1].astype(F32)
        for d in range(2):
            gate += part_in[d, i, 0].astype(F32)
            up += part_in[d, i, 1].astype(F32)
        sig = jax.nn.sigmoid(gate)
        active = gate * sig
        up_s[i] = up
        act_s[i] = active
        slope_s[i] = sig * (1.0 + gate * (1.0 - sig))
        hid[i, x] = (active * up).astype(BF)
        both_sides((hid.at[i, x], hid.at[i, x]), (hid.at[i, x], hid.at[i, x]), h_send, h_recv, i)

    def hid_pass(i):
        wait_bytes(hid.at[i, left], h_recv.at[0, i])
        wait_bytes(hid.at[i, right], h_recv.at[1, i])
        both_sides((hid.at[i, left, :, near_half],) * 2, (hid.at[i, right, :, far_half],) * 2, h2_send, h2_recv, i)

    def expert_out(i):
        wait_bytes(hid.at[i, far, :, near_half], h2_recv.at[0, i])
        wait_bytes(hid.at[i, far, :, far_half], h2_recv.at[1, i])
        prod = dot(hid[i].reshape(chip_h, CHUNK), w[2], CROSS_FIRST).astype(BF)
        rows_back[0, pl.ds(pl.multiple_of(i * GROUP, GROUP), GROUP)] = prod[0:GROUP]
        for dy in range(1, NY):
            rows_out[i, dy - 1] = prod[dy * GROUP:(dy + 1) * GROUP]

    def hidden_part(i):
        prod = dot(w[2], chunk(1, i), CROSS_LAST).astype(BF)
        for q in range(NX):
            part_h[q, i] = prod[q * quarter_h:(q + 1) * quarter_h]
        both_sides((part_h.at[far, i, :, near_half], mid_h.at[0, i]),
                   (part_h.at[far, i, :, far_half], mid_h.at[1, i]), hm_send, hm_recv, i)

    def hidden_mid(i):
        wait_bytes(mid_h.at[0, i], hm_recv.at[0, i])
        wait_bytes(mid_h.at[1, i], hm_recv.at[1, i])
        add_to(part_h.at[right, i, :, near_half], mid_h[0, i])
        add_to(part_h.at[left, i, :, far_half], mid_h[1, i])
        both_sides((part_h.at[right, i], part_h_in.at[0, i]), (part_h.at[left, i], part_h_in.at[1, i]),
                   ph_send, ph_recv, i)

    def grad_rows(i):
        for d in range(2):
            wait_bytes(part_h_in.at[d, i], ph_recv.at[d, i])
        gh = part_h[x, i].astype(F32)
        for d in range(2):
            gh += part_h_in[d, i].astype(F32)
        grads_x[i, x, 0] = (gh * up_s[i] * slope_s[i]).astype(BF)
        grads_x[i, x, 1] = (gh * act_s[i]).astype(BF)
        both_sides((grads_x.at[i, x],) * 2, (grads_x.at[i, x],) * 2, gx_send, gx_recv, i)

    def grads_pass(i):
        wait_bytes(grads_x.at[i, left], gx_recv.at[0, i])
        wait_bytes(grads_x.at[i, right], gx_recv.at[1, i])
        both_sides((grads_x.at[i, left, 0],) * 2, (grads_x.at[i, right, 1],) * 2, g2_send, g2_recv, i)

    def down_step(i):
        acc[2] += dot(hid[i].reshape(chip_h, CHUNK), chunk(1, i), PLAIN)

    def gate_step(i):
        wait_bytes(grads_x.at[i, far, 0], g2_recv.at[0, i])
        wait_bytes(grads_x.at[i, far, 1], g2_recv.at[1, i])

        def one(kind):
            acc[kind] += dot(grads_x[i, :, kind].reshape(chip_h, CHUNK), chunk(0, i), PLAIN)

        each(2, one)

    def give_back(first, count, g):
        for dy in (1, 3, 2):
            for i, off, row, n in spans(first, count):
                remote(rows_out.at[i, dy - 1, pl.ds(off, n)], rows_back.at[dy, pl.ds(row, n)],
                       o_send.at[g], o_recv.at[g], chip_at(NY - dy, 0)).start()

    def await_back(g):
        first, count = BACK[g]
        wait_bytes(rows_back.at[pl.ds(1, NY - 1), pl.ds(first, count)], o_recv.at[g])

    def dense(place):
        first = pl.multiple_of(place * SLOT // 16 * 16, 16)

        def one_y(dy):
            wts = weights(dy, place, first, WINDOW)
            coarse = wts.astype(BF)
            here = pl.ds(pl.multiple_of(dy * WINDOW, 16), WINDOW)
            back_w[0, here] = coarse
            back_w[1, here] = (wts - coarse.astype(F32)).astype(BF)

        def tile(n):
            lanes = pl.ds(pl.multiple_of(n * TILE, TILE), TILE)
            rows = rows_back[:, pl.ds(first, WINDOW), lanes].reshape(NY * WINDOW, TILE)
            sum_s[:, lanes] = dot(back_w[0], rows, CROSS_FIRST) + dot(back_w[1], rows, CROSS_FIRST)

        each(NY, one_y)
        each(feats // TILE, tile)

    def fold_send(k, d):
        src, dst = ring_out.at[d, k - 1], ring_in.at[d, k - 1]
        if k == 1:
            lanes = pl.ds(d * half_f, half_f)
            src, dst = src.at[:, lanes], dst.at[:, lanes]
        remote(src, dst, r_send.at[d, k - 1], r_recv.at[d, k - 1], chip_at(0, 1 if d == 0 else NZ - 1)).start()

    def fold_wait(k, d):
        ref = ring_in.at[d, k - 1]
        wait_bytes(ref.at[:, pl.ds(d * half_f, half_f)] if k == 1 else ref, r_recv.at[d, k - 1])

    def fold(n):
        for j, groups in ((0, (0,)), (1, (1,)), (3, (2,)), (5, (3,)), (7, (4,))):
            @pl.when(n == j)
            def _(groups=groups):
                for g in groups:
                    await_back(g)
        dense(7 - n)

        @pl.when(n == 0)
        def _():
            for d in range(2):
                ring_out[d, 0] = sum_s[...].astype(BF)
                fold_send(1, d)

        for j in range(1, 7):
            @pl.when(n == j)
            def _(k=(j + 3) // 2, d=(j - 1) % 2):
                fold_wait(k - 1, d)

        @pl.when((n >= 1) & (n <= 6))
        def _():
            k = (n + 3) // 2
            d = lax.rem(n - 1, 2)
            ring_out[d, k - 1] = (sum_s[...] + ring_in[d, k - 2].astype(F32)).astype(BF)

        for j in range(1, 7):
            @pl.when(n == j)
            def _(k=(j + 3) // 2, d=(j - 1) % 2):
                fold_send(k, d)

    def send_pair(kind):
        pair_out[kind] = acc[kind, pl.ds(pl.multiple_of((1 - c) * own_h, 16), own_h)].astype(BF)
        remote(pair_out.at[kind], pair_in.at[kind], pair_send.at[kind], pair_recv.at[kind],
               (x, sibling)).start()

    def join_pair(kind, dest):
        wait_bytes(pair_in.at[kind], pair_recv.at[kind])
        pair_in[kind] = (acc[kind, pl.ds(pl.multiple_of(c * own_h, 16), own_h)]
                         + pair_in[kind].astype(F32)).astype(BF)
        pltpu.make_async_copy(pair_in.at[kind], dest, w_loc.at[kind]).start()

    def tok_chunk(i):
        wait_bytes(xc.at[0, i], y_recv.at[0, i])
        up_gate(i)

    def cot_chunk(i):
        wait_bytes(xc.at[1, i], y_recv.at[1, i])
        hidden_part(i)

    def weights_here():
        for i, src in enumerate((wg, wu, wd)):
            wait_bytes(w_part(i, c), w_loc.at[i])
            wait_bytes(w_part(i, 1 - c), w_recv.at[i])

    for a in range(2):
        pass_on(a, 0, 32)
    for i, src in enumerate((wg, wu, wd)):
        remote(src, w_part(i, c), w_send.at[i], w_recv.at[i], (x, sibling)).start()
        pltpu.make_async_copy(src, w_part(i, c), w_loc.at[i]).start()
    each(TOK // 16, blank)
    wait_bytes(meta.at[pl.ds(1, NZ - 1)], m_recv)
    each(chip_h // 16, clear)
    weights_here()

    def during(lo, t, f):
        @pl.when((t >= lo) & (t < lo + NCH))
        def _():
            f(t - lo)

    def step(t):
        @pl.when(t < 8)
        def _():
            relay_step(t // 4, lax.rem(t, 4) + 1)

        @pl.when(t == 2)
        def _():
            ring_send(1, 1, og_in)

        during(1, t, tok_chunk)
        during(2, t, up_gate_mid)
        during(3, t, act)
        during(4, t, hid_pass)
        during(5, t, expert_out)

        @pl.when(t == 9)
        def _():
            for g, rows in enumerate(BACK):
                give_back(*rows, g)

        during(7, t, cot_chunk)
        during(8, t, hidden_mid)
        during(9, t, grad_rows)
        during(9, t, down_step)
        during(10, t, grads_pass)
        during(11, t, gate_step)

        @pl.when(t == 13)
        def _():
            send_pair(2)

        @pl.when(t == 15)
        def _():
            send_pair(0)
            send_pair(1)

        def from_step(start, n):
            return jnp.where(t >= start, n, 0)

        done = from_step(11, 1) + from_step(12, 2) + from_step(14, 2) + from_step(15, 2) + from_step(17, 1)
        due = from_step(10, 1) + from_step(11, 2) + from_step(13, 2) + from_step(14, 2) + from_step(16, 1)
        lax.fori_loop(done, due, lambda n, carry: (fold(n), carry)[1], 0)

        @pl.when(t == 16)
        def _():
            join_pair(2, g_down)
            join_pair(0, g_gate)
            join_pair(1, g_up)

    each(17, step)
    mine = sum_s[...]

    for d in range(2):
        fold_wait(4, d)
        mine += ring_in[d, 3].astype(F32)
    out[...] = mine.astype(BF)

    for i in range(3):
        wait_bytes(wg, w_send.at[i])
        wait_bytes(pair_in.at[i], w_loc.at[i])
        wait_bytes(pair_out.at[i], pair_send.at[i])
    wait_bytes(meta.at[pl.ds(1, NZ - 1)], m_send)
    for d in range(2):
        lanes = pl.ds(d * half_f, half_f)
        for k in range(1, 5):
            for a in range(2):
                wait_bytes(src_rows.at[a, 0] if k < 4 else src_rows.at[a, 0, :, lanes], z_send.at[a, d, k - 1])
            wait_bytes(ring_out.at[d, k - 1] if k > 1 else ring_out.at[d, 0, :, lanes], r_send.at[d, k - 1])
    for dy in range(1, NY):
        for a in range(2):
            wait_bytes(staged.at[a, dy, pl.ds(0, PER_Y)], y_send.at[a, dy - 1])
    for g, (first, count) in enumerate(BACK):
        wait_bytes(rows_back.at[pl.ds(1, NY - 1), pl.ds(0, count)], o_send.at[g])
    for i in range(NCH):
        for d in range(2):
            wait_bytes(mid.at[d, i], pm_send.at[d, i])
            wait_bytes(part_in.at[d, i], p_send.at[d, i])
            wait_bytes(hid.at[i, x], h_send.at[d, i])
            wait_bytes(mid_h.at[d, i], h2_send.at[d, i])
            wait_bytes(mid_h.at[d, i], hm_send.at[d, i])
            wait_bytes(part_h_in.at[d, i], ph_send.at[d, i])
            wait_bytes(grads_x.at[i, x], gx_send.at[d, i])
            wait_bytes(grads_x.at[i, x, 0], g2_send.at[d, i])


def finish_kernel(*refs):
    count = (len(refs) - 2) // 3
    results, outs, held = refs[:count], refs[count:2 * count], refs[2 * count:3 * count]
    sem_in, sem_out = refs[-2:]
    first = [pltpu.make_async_copy(results[i], held[i], sem_in.at[i]) for i in range(count)]
    last = [pltpu.make_async_copy(held[i], outs[i], sem_out.at[i]) for i in range(count)]
    for copy in first:
        copy.start()
    for i in range(count):
        first[i].wait()
        last[i].start()
    for copy in last:
        copy.wait()


def finish(results):
    anywhere = pl.BlockSpec(memory_space=pl.ANY)
    count = len(results)
    return pl.pallas_call(
        finish_kernel,
        out_shape=tuple(jax.ShapeDtypeStruct(r.shape, r.dtype) for r in results),
        in_specs=[anywhere] * count,
        out_specs=[anywhere] * count,
        scratch_shapes=[pltpu.VMEM(r.shape, r.dtype) for r in results]
        + [pltpu.SemaphoreType.DMA((count,)), pltpu.SemaphoreType.DMA((count,))],
    )(*results)


def run_layer(tokens, out_grad, ids, route, wg, wu, wd):
    own_h, feats = wg.shape
    qh = 2 * own_h // NX
    dma = pltpu.SemaphoreType.DMA
    vm = pltpu.VMEM
    scratch = [
        vm((3, 2 * own_h, feats), BF), vm((NZ + 1, 8, TOK), F32),
        vm((2, NZ + 1, TOK, feats), BF), vm((2, NCH, NY, GROUP, feats), BF),
        vm((2, NY, 4 * STEP - EARLY + STEP, feats), BF),
        vm((NY * STEP, 3 * TOK), BF), vm((NY * STEP, TOK), F32),
        vm((NX, NCH, 2, qh, CHUNK), BF), vm((2, NCH, 2, qh, CHUNK), BF), vm((2, NCH, qh, CHUNK), BF),
        vm((NCH, NX, qh, CHUNK), BF),
        vm((NX, NCH, qh, CHUNK), BF), vm((2, NCH, qh, CHUNK), BF), vm((2, NCH, qh, CHUNK // 2), BF),
        vm((NCH, NX, 2, qh, CHUNK), BF),
        vm((NCH, qh, CHUNK), F32), vm((NCH, qh, CHUNK), F32), vm((NCH, qh, CHUNK), F32),
        vm((NCH, NY - 1, GROUP, feats), BF), vm((NY, PER_Y, feats), BF),
        vm((2, NY * WINDOW, TOK), BF), vm((TOK, feats), F32),
        vm((2, 4, TOK, feats), BF), vm((2, 4, TOK, feats), BF),
        vm((3, 2 * own_h, feats), F32),
        vm((3, own_h, feats), BF), vm((3, own_h, feats), BF),
        dma((3,)), dma((3,)), dma((3,)), dma, dma, dma((2,)),
        dma((2, 2, 4)), dma((2, 2, 4)), dma((2, NY - 1)), dma((2, NCH)),
        *[dma((2, NCH))] * 16,
        dma((len(BACK),)), dma((len(BACK),)), dma((2, 4)), dma((2, 4)),
        dma((3,)), dma((3,)),
    ]
    anywhere = pl.BlockSpec(memory_space=pl.ANY)
    inside = pl.BlockSpec(memory_space=pltpu.VMEM)
    return pl.pallas_call(
        layer_kernel,
        out_shape=(
            jax.ShapeDtypeStruct((TOK, feats), BF),
            jax.ShapeDtypeStruct((own_h, feats), BF),
            jax.ShapeDtypeStruct((own_h, feats), BF),
            jax.ShapeDtypeStruct((own_h, feats), BF),
        ),
        in_specs=[anywhere] * 2 + [inside] * 2 + [anywhere] * 3,
        out_specs=[inside] + [anywhere] * 3,
        scratch_shapes=scratch,
        compiler_params=pltpu.CompilerParams(
            collective_id=0, has_side_effects=True, vmem_limit_bytes=60 * 1024 * 1024),
    )(tokens, out_grad, ids, route, wg, wu, wd)


def per_device(tokens, expert_ids, route_weights, w_gate, w_up, w_down, out_grad):
    return finish(run_layer(
        tokens, out_grad, expert_ids.T, route_weights.T, w_gate, w_up, w_down))


def solution(mesh):
    placed = (
        P("expert", "dp"),
        P("expert", None),
        P("expert", None),
        P("expert", "dp"),
        P("expert", "dp"),
        P("expert", "dp"),
        P("expert", "dp"),
    )
    return jax.shard_map(
        per_device,
        mesh=mesh,
        in_specs=placed,
        out_specs=(P("expert", "dp"), P("expert", "dp"), P("expert", "dp"), P("expert", "dp")),
        check_vma=False,
    )
```
